32 devices in a mesh: cells: 8 (over z, x), modes: 4 (over y, core).
Axes of the slice: x: 2, y: 2, z: 4, core: 2. Of those that a mesh axis runs over, the one named last changes fastest.
Arguments:
- pressure: bfloat16 [256, 8192], P('modes', 'cells'), may hold values from -6 to 6
- storage: float32 [8192], P('cells'), may hold values from 0.5 to 2
- coupling: bfloat16 [11, 256, 256], P(None, 'modes'), as said below
- transmissibility: float32 [11, 24576], P(None, 'cells'), as said below
- face_cells: int32 [2, 24576], P(None, 'cells'), may hold values from 0 to 1535, as said below
- send_list: int32 [8, 4, 128], P('cells'), may hold values from -1 to 1023, as said below
Outputs:
- first_image: bfloat16 [256, 8192], P('modes', 'cells')
- second_image: bfloat16 [256, 8192], P('modes', 'cells')
The draws below stay inside these ranges and needn't reach their ends.
Inputs may be any that keep to these rules, and one draw needn't show every extreme that they name: send_list[p, s] lists distinct owned cells of partition p, in local numbers, wanted by partition p + o_s with o = (-2, ..., -1, 1, ..., 2), followed by -1 padding; lists toward partitions outside the axis hold only -1; in every draw some list toward a lower partition and some list toward a higher partition are full. Face f of partition q joins the owned cell face_cells[0, f] with face_cells[1, f], which is a different owned cell where it is below 1024, else ghost slot s * 128 + g offset by 1024, holding entry g of send_list[q + o_s, 3 - s]; a ghost slot is named only where that entry is not -1, and every such entry is named by exactly one face. Each coupling matrix is symmetric. The first row of transmissibility is positive.
All inputs are finite; a program needn't handle non-finite values.
Results may differ from the reference program's by a relative error of at most 0.0041.
Values may be sent and summed in bfloat16 or wider, within the bound.
A program may use at most 64 MiB of HBM per device.

```python
import math
import jax
import jax.numpy as jnp
from jax import lax

CHAOS_MODES = 256
KL_TERMS = 11
CELL_DEV = 1024
GHOST_MOST = 128
REACH_PARTS = 2
FACE_DEV = 3072
NEIGHBOURS = 4
GHOST_SLOTS = 512
PARTITIONS = 8
CELLS = 8192
FACES = 24576


def ghost_plan(key):
    plan_key = jax.random.fold_in(key, 7)
    count_key, low_key, high_key = jax.random.split(plan_key, 3)
    offsets = jnp.concatenate([jnp.arange(-REACH_PARTS, 0), jnp.arange(1, REACH_PARTS + 1)]).astype(jnp.int32)
    counts = jax.random.randint(count_key, (PARTITIONS, NEIGHBOURS), GHOST_MOST // 4, GHOST_MOST + 1)
    low_full = jax.random.randint(low_key, (), REACH_PARTS, PARTITIONS)
    high_full = jax.random.randint(high_key, (), 0, PARTITIONS - REACH_PARTS)
    row_index = jnp.arange(PARTITIONS)[:, None]
    column_index = jnp.arange(NEIGHBOURS)[None, :]
    counts = jnp.where((row_index == low_full) & (column_index == 0), GHOST_MOST, counts)
    counts = jnp.where((row_index == high_full) & (column_index == NEIGHBOURS - 1), GHOST_MOST, counts)
    peer_index = row_index + offsets[None, :]
    present = (peer_index >= 0) & (peer_index < PARTITIONS)
    return (jnp.where(present, counts, 0).astype(jnp.int32), offsets)


def draw_send_list(key, part):
    counts, offsets = ghost_plan(key)
    pick_keys = jax.random.split(jax.random.fold_in(key, 11), PARTITIONS * NEIGHBOURS)
    chosen = jax.vmap(lambda one_key: jax.random.permutation(one_key, CELL_DEV)[:GHOST_MOST])(pick_keys)
    chosen = chosen.reshape(PARTITIONS, NEIGHBOURS, GHOST_MOST)
    position = jnp.arange(GHOST_MOST)[None, None, :]
    return jnp.where(position < counts[:, :, None], chosen, -1).astype(jnp.int32)


def draw_face_cells(key, part):
    counts, offsets = ghost_plan(key)
    sources = jnp.arange(PARTITIONS)[:, None] + offsets[None, :]
    present = (sources >= 0) & (sources < PARTITIONS)
    clipped = jnp.clip(sources, 0, PARTITIONS - 1)
    mirror = (NEIGHBOURS - 1 - jnp.arange(NEIGHBOURS))[None, :]
    arriving = jnp.where(present, counts[clipped, mirror], 0)
    slot_index = jnp.arange(FACE_DEV)
    block_index = jnp.minimum(slot_index // GHOST_MOST, NEIGHBOURS - 1)
    live = (slot_index[None, :] < GHOST_SLOTS) & ((slot_index % GHOST_MOST)[None, :] < arriving[:, block_index])
    face_key = jax.random.fold_in(key, 13)
    first_key, stride_key, order_key = jax.random.split(face_key, 3)
    owner_cell = jax.random.randint(first_key, (PARTITIONS, FACE_DEV), 0, CELL_DEV)
    stride = jax.random.randint(stride_key, (PARTITIONS, FACE_DEV), 1, CELL_DEV)
    other_cell = jnp.where(live, CELL_DEV + slot_index[None, :], (owner_cell + stride) % CELL_DEV)
    order_keys = jax.random.split(order_key, PARTITIONS)
    orders = jax.vmap(lambda one_key: jax.random.permutation(one_key, FACE_DEV))(order_keys)
    owner_cell = jnp.take_along_axis(owner_cell, orders, axis=1)
    other_cell = jnp.take_along_axis(other_cell, orders, axis=1)
    return jnp.stack([owner_cell, other_cell], 0).reshape(2, FACES).astype(jnp.int32)


def draw_transmissibility(key, part):
    mean_key, term_key = jax.random.split(jax.random.fold_in(key, 17))
    mean_part = 0.25 * jnp.exp(jax.random.uniform(mean_key, (1, FACES), minval=-1.0, maxval=1.0))
    relative = 0.6 * jnp.clip(jax.random.normal(term_key, (KL_TERMS - 1, FACES)), -4.0, 4.0)
    return jnp.concatenate([mean_part, mean_part * relative], 0).astype(jnp.float32)


def draw_coupling(key, part):
    draw_key = jax.random.fold_in(key, 19)
    entries = jax.random.normal(draw_key, (KL_TERMS, CHAOS_MODES, CHAOS_MODES))
    symmetric = (entries + jnp.swapaxes(entries, 1, 2)) * (0.7071068 * 0.35 / math.sqrt(CHAOS_MODES))
    term_index = jnp.arange(KL_TERMS)[:, None, None]
    row_index = jnp.arange(CHAOS_MODES)[None, :, None]
    column_index = jnp.arange(CHAOS_MODES)[None, None, :]
    identity_part = jnp.where((term_index == 0) & (row_index == column_index), 1.0, 0.0)
    return (symmetric + identity_part).astype(jnp.bfloat16)


def shard_levels(key, extent, cuts, low, high):
    loudness = 1.0
    for dim, shards_of in cuts:
        heights = jax.random.uniform(jax.random.fold_in(jax.random.fold_in(key, 6), dim), (shards_of,), jnp.float32, low / len(cuts), high / len(cuts))
        loudness = loudness * jnp.repeat(jnp.exp(heights), extent[dim] // shards_of).reshape((-1,) + (1,) * (len(extent) - 1 - dim))
    return loudness


def scatter_about(stream_key, extent, deviation, most, cuts=(), held_as=jnp.bfloat16):
    values = jax.random.normal(stream_key, extent, jnp.float32) * deviation
    if len(cuts) > 0:
        values = shard_levels(stream_key, extent, cuts, -0.22, 0.18) * values
    return jnp.clip(values, min=-most, max=most).astype(held_as)


def setup_inputs(seed: int = 0) -> dict:
    arg_keys = jax.random.split(jax.random.key(seed), 7)
    pressure = scatter_about(arg_keys[0], (CHAOS_MODES, CELLS), 1.0, 6.0, ((0, 4), (1, 8)))
    storage = jnp.clip(jnp.exp(math.log(2.0) - 1.3862944 * jax.random.uniform(arg_keys[1], (CELLS,), jnp.float32) ** shard_levels(arg_keys[1], (CELLS,), ((0, 8),), -0.2, 0.2)), 0.5, 2.0)
    coupling = draw_coupling(jax.random.fold_in(arg_keys[6], 71), 0)
    transmissibility = draw_transmissibility(jax.random.fold_in(arg_keys[6], 71), 0)
    face_cells = draw_face_cells(jax.random.fold_in(arg_keys[6], 71), 0)
    send_list = draw_send_list(jax.random.fold_in(arg_keys[6], 71), 0)
    return {"pressure": pressure, "storage": storage, "coupling": coupling, "transmissibility": transmissibility, "face_cells": face_cells, "send_list": send_list}


def apply_whole(field, storage, coupling, transmissibility, face_cells, send_list, offsets):
    blocks = jnp.transpose(field.reshape(CHAOS_MODES, PARTITIONS, CELL_DEV), (1, 0, 2))
    coupling_wide = coupling.astype(jnp.float32)
    mirror = (NEIGHBOURS - 1 - jnp.arange(NEIGHBOURS)).astype(jnp.int32)

    def one_partition(partition):
        sources = partition + offsets
        present = (sources >= 0) & (sources < PARTITIONS)
        clipped = jnp.clip(sources, 0, PARTITIONS - 1).astype(jnp.int32)
        wanted = send_list[clipped, mirror]
        usable = present[:, None] & (wanted >= 0)
        cells_from = blocks[clipped]
        safe_cells = jnp.maximum(wanted, 0).astype(jnp.int32)
        picked = jnp.take_along_axis(cells_from, safe_cells[:, None, :], axis=2)
        picked = jnp.where(usable[:, None, :], picked, jnp.zeros((), field.dtype))
        ghosts = jnp.transpose(picked, (1, 0, 2)).reshape(CHAOS_MODES, GHOST_SLOTS)
        owned = blocks[partition]
        extended = jnp.concatenate([owned, ghosts], axis=1).astype(jnp.float32)
        face_rows = lax.dynamic_slice_in_dim(face_cells, (partition * FACE_DEV).astype(jnp.int32), FACE_DEV, 1)
        face_weights = lax.dynamic_slice_in_dim(transmissibility, (partition * FACE_DEV).astype(jnp.int32), FACE_DEV, 1)
        local_storage = lax.dynamic_slice_in_dim(storage, (partition * CELL_DEV).astype(jnp.int32), CELL_DEV, 0)
        owner_cell = face_rows[0]
        other_cell = face_rows[1]
        inner_cell = jnp.where(other_cell < CELL_DEV, other_cell, CELL_DEV)

        def add_term(running, term_index):
            mixed_field = jnp.dot(coupling_wide[term_index], extended, precision=lax.Precision.HIGHEST)
            fluxes = face_weights[term_index][None, :] * (mixed_field[:, owner_cell] - mixed_field[:, other_cell])
            running = running.at[:, owner_cell].add(fluxes)
            running = running.at[:, inner_cell].add(-fluxes, mode="drop")
            return running, None

        storage_term = local_storage[None, :] * owned.astype(jnp.float32)
        running, unused = lax.scan(add_term, storage_term, jnp.arange(KL_TERMS).astype(jnp.int32))
        return running

    result = lax.map(one_partition, jnp.arange(PARTITIONS).astype(jnp.int32))
    return jnp.transpose(result, (1, 0, 2)).reshape(CHAOS_MODES, CELLS)


def reference(pressure, storage, coupling, transmissibility, face_cells, send_list):
    offsets = jnp.concatenate([jnp.arange(-REACH_PARTS, 0), jnp.arange(1, REACH_PARTS + 1)]).astype(jnp.int32)
    first_image = apply_whole(pressure, storage, coupling, transmissibility, face_cells, send_list, offsets).astype(jnp.bfloat16)
    second_image = apply_whole(first_image, storage, coupling, transmissibility, face_cells, send_list, offsets).astype(jnp.bfloat16)
    return first_image, second_image
```

```python
import functools

import jax
import jax.numpy as jnp
from jax import lax
from jax.experimental import pallas as pl
from jax.experimental.pallas import tpu as pltpu
from jax.sharding import PartitionSpec as P

MESH = pl.DeviceIdType.MESH
BLOCK = 256
TILE = 512
AHEAD = 2


def onehot(rows, base, index_row, dtype=jnp.bfloat16):
    near = jnp.clip(index_row - base, -1, rows).astype(jnp.float32).astype(jnp.bfloat16)
    iota = lax.broadcasted_iota(jnp.int32, (rows, index_row.shape[1]), 0)
    return iota.astype(jnp.float32).astype(jnp.bfloat16) == near


def kernel(
    parts, groups, pressure, storage_in, coupling_in, trans_in, faces_in, sends_in, first, second,
    storage, coupling, trans, faces, sends,
    wide, ghost_hot, picked_rows, fields, sums, totals, flux, out_w, in_w, out_t, in_t, slot_owner,
    load, near_send, near_recv, far_send, far_recv, pass_send, pass_recv,
    w_send, w_recv, t_send, t_recv,
):
    rows, cells = pressure.shape
    terms = coupling.shape[0]
    face_count = faces.shape[1]
    lists, width = sends.shape[1:]
    ghosts = lists * width
    reach = lists // 2
    offsets = list(range(-reach, 0)) + list(range(1, reach + 1))
    chunks = cells // BLOCK
    part = lax.axis_index("cells")
    group = lax.axis_index("modes")
    partner = group + 1 - 2 * lax.rem(group, 2)
    far = lax.rem(group + 2, 4)
    far_partner = lax.rem(partner + 2, 4)

    def band(member):
        return pl.ds(pl.multiple_of(member * rows, rows), rows)

    mine = band(group)
    one = jnp.ones((), jnp.bfloat16)
    zero = jnp.zeros((), jnp.bfloat16)

    def present(slot):
        return jnp.logical_and(part + offsets[slot] >= 0, part + offsets[slot] < parts)

    def band_copy(app, chunk, member, send_sem, recv_sem, target):
        return pltpu.make_async_remote_copy(
            src_ref=fields.at[app, chunk, band(member)],
            dst_ref=fields.at[app, chunk, band(member)],
            send_sem=send_sem.at[app, chunk],
            recv_sem=recv_sem.at[app, chunk],
            device_id={"modes": target},
            device_id_type=MESH,
        )

    def near_copy(app, chunk, member=group):
        return band_copy(app, chunk, member, near_send, near_recv, partner)

    def far_copy(app, chunk, member=group):
        return band_copy(app, chunk, member, far_send, far_recv, far)

    def pass_copy(app, chunk, member=far):
        return band_copy(app, chunk, member, pass_send, pass_recv, partner)

    def flux_copy(app, slot):
        return pltpu.make_async_remote_copy(
            src_ref=out_w.at[app, slot],
            dst_ref=in_w.at[app, lists - 1 - slot],
            send_sem=w_send.at[app, slot],
            recv_sem=w_recv.at[app, lists - 1 - slot],
            device_id={"cells": part + offsets[slot]},
            device_id_type=MESH,
        )

    def flux_wait(app, slot):
        return pltpu.make_async_remote_copy(
            src_ref=out_w.at[app, lists - 1 - slot],
            dst_ref=in_w.at[app, slot],
            send_sem=w_send.at[app, lists - 1 - slot],
            recv_sem=w_recv.at[app, slot],
            device_id={"cells": part + offsets[slot]},
            device_id_type=MESH,
        )

    def weight_copy(slot):
        return pltpu.make_async_remote_copy(
            src_ref=out_t.at[slot],
            dst_ref=in_t.at[lists - 1 - slot],
            send_sem=t_send.at[slot],
            recv_sem=t_recv.at[lists - 1 - slot],
            device_id={"cells": part + offsets[slot]},
            device_id_type=MESH,
        )

    def weight_wait(slot):
        return pltpu.make_async_remote_copy(
            src_ref=out_t.at[lists - 1 - slot],
            dst_ref=in_t.at[slot],
            send_sem=t_send.at[lists - 1 - slot],
            recv_sem=t_recv.at[slot],
            device_id={"cells": part + offsets[slot]},
            device_id_type=MESH,
        )

    loads = [
        pltpu.make_async_copy(
            pressure.at[:, chunk * BLOCK:(chunk + 1) * BLOCK], fields.at[0, chunk, mine], load.at[chunk]
        )
        for chunk in range(chunks)
    ]
    for index, (source, target) in enumerate(
        ((faces_in, faces), (trans_in, trans), (sends_in, sends), (storage_in, storage),
         (coupling_in, coupling))
    ):
        loads.append(pltpu.make_async_copy(source, target, load.at[chunks + index]))
    for copy in loads:
        copy.start()
    in_w[...] = jnp.zeros_like(in_w)
    in_t[...] = jnp.zeros_like(in_t)
    barrier = pltpu.get_barrier_semaphore()
    for peer in (partner, far):
        pl.semaphore_signal(barrier, inc=1, device_id={"modes": peer}, device_id_type=MESH)
    peers = 2
    for slot in range(lists):
        peers = peers + present(slot).astype(jnp.int32)

        @pl.when(present(slot))
        def _():
            pl.semaphore_signal(
                barrier, inc=1, device_id={"cells": part + offsets[slot]}, device_id_type=MESH
            )
    for chunk in range(chunks):
        loads[chunk].wait()
    pl.semaphore_wait(barrier, peers)
    for chunk in range(chunks):
        far_copy(0, chunk).start()
        near_copy(0, chunk).start()
    for copy in loads[chunks:]:
        copy.wait()

    t = trans[...]
    t_high = t.astype(jnp.bfloat16)
    t_low = (t - t_high.astype(jnp.float32)).astype(jnp.bfloat16)
    picked_rows[...] = jnp.zeros_like(picked_rows)
    picked_rows[0:terms] = t_high
    picked_rows[16:16 + terms] = t_low
    owner = faces[0:1]
    owner_next = owner + 1
    picked_rows[32:33] = (owner_next // 32).astype(jnp.float32).astype(jnp.bfloat16)
    picked_rows[33:34] = (owner_next % 32).astype(jnp.float32).astype(jnp.bfloat16)

    def build_ghost(index, carry):
        at = pl.ds(pl.multiple_of(index * TILE, TILE), TILE)
        other = faces[1:2, at]
        for base in range(0, ghosts, BLOCK):
            hot = onehot(BLOCK, cells + base, other)
            ghost_hot[base:base + BLOCK, at] = jnp.where(hot, one, zero)
        return carry

    lax.fori_loop(0, face_count // TILE, build_ghost, 0)
    found = lax.dot_general(
        picked_rows[...], ghost_hot[...], (((1,), (1,)), ((), ())), preferred_element_type=jnp.float32
    )
    weights = found[0:16] + found[16:32]
    slot_owner[0:1] = (found[32:33] * 32.0 + found[33:34] - 1.0).astype(jnp.int32)
    for slot in range(lists):
        out_t[slot] = weights[:, slot * width:(slot + 1) * width]

        @pl.when(present(slot))
        def _():
            weight_copy(slot).start()

    def build_block(base):
        for slot in range(lists):
            hot = onehot(BLOCK, base, sends[0, slot:slot + 1])
            wide[base:base + BLOCK, slot * width:(slot + 1) * width] = jnp.where(hot, one, zero)

        def build_faces(index, carry):
            at = pl.ds(pl.multiple_of(index * TILE, TILE), TILE)
            to = pl.ds(pl.multiple_of(ghosts + index * TILE, TILE), TILE)
            plus = onehot(BLOCK, base, faces[0:1, at])
            minus = onehot(BLOCK, base, faces[1:2, at])
            wide[base:base + BLOCK, to] = jnp.where(plus, one, jnp.where(minus, -one, zero))
            return carry

        lax.fori_loop(0, face_count // TILE, build_faces, 0)
        hot = onehot(BLOCK, base, slot_owner[0:1])
        wide[base:base + BLOCK, ghosts + face_count:] = jnp.where(hot, -one, zero)

    tiles = [(start, min(TILE, ghosts + face_count - start)) for start in range(0, ghosts + face_count, TILE)]

    def across(app, chunk, start, size):
        rows_of = slice(chunk * BLOCK, (chunk + 1) * BLOCK)
        part_sum = jnp.dot(
            fields[app, chunk], wide[rows_of, start:start + size], preferred_element_type=jnp.float32
        )
        return part_sum if chunk == 0 else sums[:, start:start + size] + part_sum

    def mix(app, start, size, weights):
        column = across(app, chunks - 1, start, size).astype(jnp.bfloat16)
        stacked = coupling[...].reshape(terms * rows, groups * rows)
        mixed = jnp.dot(stacked, column, preferred_element_type=jnp.float32)
        total = mixed[0:rows] * weights[0:1]
        for term in range(1, terms):
            total += mixed[term * rows:(term + 1) * rows] * weights[term:term + 1]
        return total

    for app, target in enumerate((first, second)):
        for chunk in range(chunks + 1):
            if chunk < chunks:
                if app == 0:
                    build_block(chunk * BLOCK)
                far_copy(app, chunk, far).wait_recv()
                pass_copy(app, chunk).start()
            if chunk > 0:
                near_copy(app, chunk - 1, partner).wait_recv()
                pass_copy(app, chunk - 1, far_partner).wait_recv()
                if chunk < chunks:
                    for start, size in tiles:
                        sums[:, start:start + size] = across(app, chunk - 1, start, size)
        if app == 0:
            for slot in range(lists):
                @pl.when(present(slot))
                def _():
                    weight_wait(slot).wait_recv()
        sent_weights = jnp.concatenate([in_t[slot] for slot in range(lists)], axis=1)
        sent = mix(app, 0, ghosts, sent_weights)
        for slot in range(lists):
            out_w[app, slot] = sent[:, slot * width:(slot + 1) * width].astype(jnp.bfloat16)

            @pl.when(present(slot))
            def _():
                flux_copy(app, slot).start()

        for start in range(0, face_count, TILE):
            at = slice(start, start + TILE)
            total = mix(app, ghosts + start, TILE, trans[:, at])
            high = total.astype(jnp.bfloat16)
            flux[0:rows, at] = high
            flux[rows:2 * rows, at] = (total - high.astype(jnp.float32)).astype(jnp.bfloat16)

        def inner(chunk):
            span = slice(chunk * BLOCK, (chunk + 1) * BLOCK)
            spread = lax.dot_general(
                flux[...], wide[span, ghosts:ghosts + face_count], (((1,), (1,)), ((), ())),
                preferred_element_type=jnp.float32,
            )
            image = storage[:, span] * fields[app, chunk, mine, :].astype(jnp.float32)
            return image + spread[0:rows] + spread[rows:2 * rows]

        def finish(chunk, image, arrived):
            span = slice(chunk * BLOCK, (chunk + 1) * BLOCK)
            spread = lax.dot_general(
                arrived, wide[span, ghosts + face_count:], (((1,), (1,)), ((), ())),
                preferred_element_type=jnp.float32,
            )
            image = (image + spread).astype(jnp.bfloat16)
            target[:, span] = image
            if app == 0:
                fields[1, chunk, mine, :] = image
                far_copy(1, chunk).start()
                near_copy(1, chunk).start()

        ahead = min(AHEAD, chunks)
        for chunk in range(ahead):
            totals[:, chunk * BLOCK:(chunk + 1) * BLOCK] = inner(chunk)
        for slot in range(lists):
            @pl.when(present(slot))
            def _():
                flux_wait(app, slot).wait_recv()
        arrived = jnp.concatenate([in_w[app, slot] for slot in range(lists)], axis=1)
        for chunk in range(ahead):
            finish(chunk, totals[:, chunk * BLOCK:(chunk + 1) * BLOCK], arrived)
        for chunk in range(ahead, chunks):
            finish(chunk, inner(chunk), arrived)

    for app in range(2):
        for chunk in range(chunks):
            far_copy(app, chunk).wait_send()
            near_copy(app, chunk).wait_send()
            pass_copy(app, chunk).wait_send()
    for slot in range(lists):
        @pl.when(present(slot))
        def _():
            weight_copy(slot).wait_send()
            for app in range(2):
                flux_copy(app, slot).wait_send()


def write_out(first_in, second_in, first, second, done):
    copies = [
        pltpu.make_async_copy(source, target, done.at[index])
        for index, (source, target) in enumerate(((first_in, first), (second_in, second)))
    ]
    for copy in copies:
        copy.start()
    for copy in copies:
        copy.wait()


def local(parts, groups, pressure, storage, coupling, trans, face_cells, send_list):
    assert groups == 4
    rows, cells = pressure.shape
    face_count = face_cells.shape[1]
    lists, width = send_list.shape[1:]
    ghosts = lists * width
    chunks = cells // BLOCK
    bf16 = jnp.bfloat16
    vmem = pl.BlockSpec(memory_space=pltpu.VMEM)
    image = jax.ShapeDtypeStruct((rows, cells), bf16)
    images = pl.pallas_call(
        functools.partial(kernel, parts, groups),
        out_shape=(pltpu.VMEM((rows, cells), bf16), pltpu.VMEM((rows, cells), bf16)),
        in_specs=[pl.BlockSpec(memory_space=pltpu.HBM)] * 6,
        out_specs=(vmem, vmem),
        scratch_shapes=[
            pltpu.VMEM((1, cells), jnp.float32),
            pltpu.VMEM(coupling.shape, bf16),
            pltpu.VMEM(trans.shape, jnp.float32),
            pltpu.VMEM(face_cells.shape, jnp.int32),
            pltpu.VMEM(send_list.shape, jnp.int32),
            pltpu.VMEM((cells, 2 * ghosts + face_count), bf16),
            pltpu.VMEM((ghosts, face_count), bf16),
            pltpu.VMEM((48, face_count), bf16),
            pltpu.VMEM((2, chunks, groups * rows, BLOCK), bf16),
            pltpu.VMEM((groups * rows, ghosts + face_count), jnp.float32),
            pltpu.VMEM((rows, cells), jnp.float32),
            pltpu.VMEM((2 * rows, face_count), bf16),
            pltpu.VMEM((2, lists, rows, width), bf16),
            pltpu.VMEM((2, lists, rows, width), bf16),
            pltpu.VMEM((lists, 16, width), jnp.float32),
            pltpu.VMEM((lists, 16, width), jnp.float32),
            pltpu.VMEM((8, ghosts), jnp.int32),
            pltpu.SemaphoreType.DMA((chunks + 5,)),
        ]
        + [pltpu.SemaphoreType.DMA((2, chunks))] * 6
        + [pltpu.SemaphoreType.DMA((2, lists))] * 2
        + [pltpu.SemaphoreType.DMA((lists,))] * 2,
        compiler_params=pltpu.CompilerParams(
            collective_id=0, has_side_effects=True, vmem_limit_bytes=61 * 1024 * 1024
        ),
    )(pressure, storage.reshape(1, cells), coupling, trans, face_cells, send_list)
    hbm = pl.BlockSpec(memory_space=pltpu.HBM)
    return pl.pallas_call(
        write_out,
        out_shape=(image, image),
        in_specs=[vmem] * 2,
        out_specs=(hbm, hbm),
        scratch_shapes=[pltpu.SemaphoreType.DMA((2,))],
        compiler_params=pltpu.CompilerParams(vmem_limit_bytes=1024 * 1024),
    )(*images)


def solution(mesh):
    placed = (
        P("modes", "cells"),
        P("cells"),
        P(None, "modes", None),
        P(None, "cells"),
        P(None, "cells"),
        P("cells", None, None),
    )
    return jax.shard_map(
        functools.partial(local, mesh.shape["cells"], mesh.shape["modes"]),
        mesh=mesh,
        in_specs=placed,
        out_specs=(P("modes", "cells"), P("modes", "cells")),
        check_vma=False,
    )
```

```python
import functools

import jax
import jax.numpy as jnp
from jax import lax
from jax.experimental import pallas as pl
from jax.experimental.pallas import tpu as pltpu
from jax.sharding import PartitionSpec as P

MESH = pl.DeviceIdType.MESH
BLOCK = 256
TILE = 512


def onehot(rows, base, index_row, dtype=jnp.bfloat16):
    near = jnp.clip(index_row - base, -1, rows).astype(jnp.float32).astype(jnp.bfloat16)
    iota = lax.broadcasted_iota(jnp.int32, (rows, index_row.shape[1]), 0)
    return iota.astype(jnp.float32).astype(jnp.bfloat16) == near


def kernel(
    parts, groups, pressure, storage_in, coupling_in, trans_in, faces_in, sends_in, first, second,
    storage, coupling, trans, faces, sends, pair, turned,
    wide, tall, ghost_hot, picked_rows, fields, sums, diff, totals, flux, out_w, in_w, out_t, in_t, slot_owner, ghost,
    load, near_send, near_recv, far_send, far_recv, pass_send, pass_recv,
    w_send, w_recv, t_send, t_recv, pair_send, pair_recv,
):
    rows, cells = pressure.shape
    terms = coupling.shape[0]
    face_count = faces.shape[1]
    lists, width = sends.shape[1:]
    ghosts = lists * width
    reach = lists // 2
    offsets = list(range(-reach, 0)) + list(range(1, reach + 1))
    chunks = cells // BLOCK
    part = lax.axis_index("cells")
    group = lax.axis_index("modes")
    partner = group + 1 - 2 * lax.rem(group, 2)
    far = lax.rem(group + 2, 4)
    far_partner = lax.rem(partner + 2, 4)

    def band(member):
        return pl.ds(pl.multiple_of(member * rows, rows), rows)

    mine = band(group)
    one = jnp.ones((), jnp.bfloat16)
    zero = jnp.zeros((), jnp.bfloat16)

    def present(slot):
        return jnp.logical_and(part + offsets[slot] >= 0, part + offsets[slot] < parts)

    def band_copy(app, chunk, member, send_sem, recv_sem, target):
        return pltpu.make_async_remote_copy(
            src_ref=fields.at[app, chunk, band(member)],
            dst_ref=fields.at[app, chunk, band(member)],
            send_sem=send_sem.at[app, chunk],
            recv_sem=recv_sem.at[app, chunk],
            device_id={"modes": target},
            device_id_type=MESH,
        )

    def near_copy(app, chunk, member=group):
        return band_copy(app, chunk, member, near_send, near_recv, partner)

    def far_copy(app, chunk, member=group):
        return band_copy(app, chunk, member, far_send, far_recv, far)

    def pass_copy(app, chunk, member=far):
        return band_copy(app, chunk, member, pass_send, pass_recv, partner)

    def flux_peer(side, slot):
        peer = part + offsets[slot]
        return {"cells": peer} if side == 0 else {"cells": peer, "modes": far}

    def flux_copy(app, side, slot):
        return pltpu.make_async_remote_copy(
            src_ref=out_w.at[app, side, slot],
            dst_ref=in_w.at[app, side, lists - 1 - slot],
            send_sem=w_send.at[app, side, slot],
            recv_sem=w_recv.at[app, side, lists - 1 - slot],
            device_id=flux_peer(side, slot),
            device_id_type=MESH,
        )

    def flux_wait(app, side, slot):
        return pltpu.make_async_remote_copy(
            src_ref=out_w.at[app, side, lists - 1 - slot],
            dst_ref=in_w.at[app, side, slot],
            send_sem=w_send.at[app, side, lists - 1 - slot],
            recv_sem=w_recv.at[app, side, slot],
            device_id=flux_peer(side, slot),
            device_id_type=MESH,
        )

    def pair_copy(member):
        at = pl.ds(pl.multiple_of(lax.rem(member, 2) * rows, rows), rows)
        return pltpu.make_async_remote_copy(
            src_ref=pair.at[:, at],
            dst_ref=pair.at[:, at],
            send_sem=pair_send.at[0],
            recv_sem=pair_recv.at[0],
            device_id={"modes": partner},
            device_id_type=MESH,
        )

    def weight_copy(slot):
        return pltpu.make_async_remote_copy(
            src_ref=out_t.at[slot],
            dst_ref=in_t.at[lists - 1 - slot],
            send_sem=t_send.at[slot],
            recv_sem=t_recv.at[lists - 1 - slot],
            device_id={"cells": part + offsets[slot]},
            device_id_type=MESH,
        )

    def weight_wait(slot):
        return pltpu.make_async_remote_copy(
            src_ref=out_t.at[lists - 1 - slot],
            dst_ref=in_t.at[slot],
            send_sem=t_send.at[lists - 1 - slot],
            recv_sem=t_recv.at[slot],
            device_id={"cells": part + offsets[slot]},
            device_id_type=MESH,
        )

    loads = [
        pltpu.make_async_copy(
            pressure.at[:, chunk * BLOCK:(chunk + 1) * BLOCK], fields.at[0, chunk, mine], load.at[chunk]
        )
        for chunk in range(chunks)
    ]
    for index, (source, target) in enumerate(
        ((faces_in, faces), (trans_in, trans), (sends_in, sends), (storage_in, storage),
         (coupling_in, pair.at[:, pl.ds(pl.multiple_of(lax.rem(group, 2) * rows, rows), rows)]),
         (coupling_in, coupling))
    ):
        loads.append(pltpu.make_async_copy(source, target, load.at[chunks + index]))
    for copy in loads:
        copy.start()
    in_w[...] = jnp.zeros_like(in_w)
    in_t[...] = jnp.zeros_like(in_t)
    barrier = pltpu.get_barrier_semaphore()
    for peer in (partner, far):
        pl.semaphore_signal(barrier, inc=1, device_id={"modes": peer}, device_id_type=MESH)
    peers = 2
    for slot in range(lists):
        peers = peers + 2 * present(slot).astype(jnp.int32)

        @pl.when(present(slot))
        def _():
            pl.semaphore_signal(
                barrier, inc=1, device_id={"cells": part + offsets[slot]}, device_id_type=MESH
            )
            pl.semaphore_signal(
                barrier, inc=1, device_id={"cells": part + offsets[slot], "modes": far}, device_id_type=MESH
            )
    for copy in loads:
        copy.wait()

    t = trans[...]
    t_high = t.astype(jnp.bfloat16)
    t_low = (t - t_high.astype(jnp.float32)).astype(jnp.bfloat16)
    picked_rows[...] = jnp.zeros_like(picked_rows)
    picked_rows[0:terms] = t_high
    picked_rows[16:16 + terms] = t_low
    owner = faces[0:1]
    owner_next = owner + 1
    picked_rows[32:33] = (owner_next // 32).astype(jnp.float32).astype(jnp.bfloat16)
    picked_rows[33:34] = (owner_next % 32).astype(jnp.float32).astype(jnp.bfloat16)

    def build_ghost(index, carry):
        at = pl.ds(pl.multiple_of(index * TILE, TILE), TILE)
        other = faces[1:2, at]
        for base in range(0, ghosts, BLOCK):
            hot = onehot(BLOCK, cells + base, other)
            ghost_hot[base:base + BLOCK, at] = jnp.where(hot, one, zero)
        return carry

    lax.fori_loop(0, face_count // TILE, build_ghost, 0)
    found = lax.dot_general(
        picked_rows[...], ghost_hot[...], (((1,), (1,)), ((), ())), preferred_element_type=jnp.float32
    )
    weights = found[0:16] + found[16:32]
    slot_owner[0:1] = (found[32:33] * 32.0 + found[33:34] - 1.0).astype(jnp.int32)
    for slot in range(lists):
        out_t[slot] = weights[:, slot * width:(slot + 1) * width]
    pl.semaphore_wait(barrier, peers)
    for chunk in range(chunks):
        far_copy(0, chunk).start()
        near_copy(0, chunk).start()
    for slot in range(lists):
        @pl.when(present(slot))
        def _():
            weight_copy(slot).start()
    pair_copy(group).start()

    def build_block(base):
        for slot in range(lists):
            hot = onehot(BLOCK, base, sends[0, slot:slot + 1])
            wide[base:base + BLOCK, slot * width:(slot + 1) * width] = jnp.where(hot, one, zero)

        def build_faces(index, carry):
            at = pl.ds(pl.multiple_of(index * TILE, TILE), TILE)
            to = pl.ds(pl.multiple_of(ghosts + index * TILE, TILE), TILE)
            plus = onehot(BLOCK, base, faces[0:1, at])
            minus = onehot(BLOCK, base, faces[1:2, at])
            signs = jnp.where(plus, one, jnp.where(minus, -one, zero))
            wide[base:base + BLOCK, to] = signs
            tall[at, base:base + BLOCK] = signs.T
            return carry

        lax.fori_loop(0, face_count // TILE, build_faces, 0)
        hot = onehot(BLOCK, base, slot_owner[0:1])
        tall[face_count:, base:base + BLOCK] = jnp.where(hot, -one, zero).T


    half = 2 * rows
    near_half = pl.ds(pl.multiple_of(lax.div(group, 2) * half, half), half)
    far_half = pl.ds(pl.multiple_of((1 - lax.div(group, 2)) * half, half), half)

    def differ(app, chunk, members):
        rows_of = slice(chunk * BLOCK, (chunk + 1) * BLOCK)
        field = fields[app, chunk, members]
        for start in range(0, face_count, TILE):
            at = slice(start, start + TILE)
            total = jnp.dot(
                field, wide[rows_of, ghosts + start:ghosts + start + TILE], preferred_element_type=jnp.float32
            )
            if chunk > 0:
                total += sums[:, at]
            if chunk < chunks - 1:
                sums[:, at] = total
            else:
                diff[members, at] = total.astype(jnp.bfloat16)

    def pick(app):
        total = jnp.dot(fields[app, 0, near_half], wide[0:BLOCK, 0:ghosts], preferred_element_type=jnp.float32)
        for chunk in range(1, chunks):
            total += jnp.dot(
                fields[app, chunk, near_half], wide[chunk * BLOCK:(chunk + 1) * BLOCK, 0:ghosts],
                preferred_element_type=jnp.float32,
            )
        ghost[...] = total.astype(jnp.bfloat16)

    def mix(stacked, column, weights):
        mixed = jnp.dot(stacked, column, preferred_element_type=jnp.float32)
        total = mixed[0:rows] * weights[0:1]
        for term in range(1, terms):
            total += mixed[term * rows:(term + 1) * rows] * weights[term:term + 1]
        return total

    for chunk in range(chunks):
        build_block(chunk * BLOCK)
    pair_copy(partner).wait_recv()

    def turn(term, carry):
        turned[term] = pair[term].T
        return carry

    lax.fori_loop(0, terms, turn, 0)
    for app, target in enumerate((first, second)):
        for chunk in range(chunks):
            near_copy(app, chunk, partner).wait_recv()
        pick(app)
        if app == 0:
            for slot in range(lists):
                @pl.when(present(slot))
                def _():
                    weight_wait(slot).wait_recv()
        sent_weights = jnp.concatenate([in_t[slot] for slot in range(lists)], axis=1)
        for side, member in enumerate((group, far)):
            sent = mix(turned[:, band(member)].reshape(terms * rows, half), ghost[...], sent_weights)
            for slot in range(lists):
                out_w[app, side, slot] = sent[:, slot * width:(slot + 1) * width].astype(jnp.bfloat16)
        for slot in range(lists):
            @pl.when(present(slot))
            def _():
                for side in (1, 0):
                    flux_copy(app, side, slot).start()
        for chunk in range(chunks):
            far_copy(app, chunk, far).wait_recv()
            pass_copy(app, chunk).start()
            differ(app, chunk, near_half)
        for chunk in range(chunks):
            pass_copy(app, chunk, far_partner).wait_recv()
            differ(app, chunk, far_half)

        stacked = coupling[...].reshape(terms * rows, groups * rows)
        for start in range(0, face_count, TILE):
            at = slice(start, start + TILE)
            total = mix(stacked, diff[:, at], trans[:, at])
            high = total.astype(jnp.bfloat16)
            flux[0:rows, at] = high
            flux[rows:2 * rows, at] = (total - high.astype(jnp.float32)).astype(jnp.bfloat16)

        for chunk in range(chunks):
            span = slice(chunk * BLOCK, (chunk + 1) * BLOCK)
            spread = jnp.dot(flux[...], tall[0:face_count, span], preferred_element_type=jnp.float32)
            image = storage[:, span] * fields[app, chunk, mine, :].astype(jnp.float32)
            totals[:, span] = image + spread[0:rows] + spread[rows:2 * rows]
        for slot in range(lists):
            @pl.when(present(slot))
            def _():
                for side in range(2):
                    flux_wait(app, side, slot).wait_recv()
        arrived = jnp.concatenate(
            [jnp.concatenate([in_w[app, side, slot] for slot in range(lists)], axis=1) for side in range(2)], axis=0
        )
        for chunk in range(chunks):
            span = slice(chunk * BLOCK, (chunk + 1) * BLOCK)
            spread = jnp.dot(arrived, tall[face_count:, span], preferred_element_type=jnp.float32)
            image = (totals[:, span] + (spread[0:rows] + spread[rows:half])).astype(jnp.bfloat16)
            target[:, span] = image
            if app == 0:
                fields[1, chunk, mine, :] = image
                far_copy(1, chunk).start()
                near_copy(1, chunk).start()

    for app in range(2):
        for chunk in range(chunks):
            far_copy(app, chunk).wait_send()
            near_copy(app, chunk).wait_send()
            pass_copy(app, chunk).wait_send()
    for slot in range(lists):
        @pl.when(present(slot))
        def _():
            weight_copy(slot).wait_send()
            for app in range(2):
                for side in range(2):
                    flux_copy(app, side, slot).wait_send()
    pair_copy(group).wait_send()


def write_out(first_in, second_in, first, second, done):
    copies = [
        pltpu.make_async_copy(source, target, done.at[index])
        for index, (source, target) in enumerate(((first_in, first), (second_in, second)))
    ]
    for copy in copies:
        copy.start()
    for copy in copies:
        copy.wait()


def local(parts, groups, pressure, storage, coupling, trans, face_cells, send_list):
    assert groups == 4
    rows, cells = pressure.shape
    face_count = face_cells.shape[1]
    lists, width = send_list.shape[1:]
    ghosts = lists * width
    chunks = cells // BLOCK
    bf16 = jnp.bfloat16
    vmem = pl.BlockSpec(memory_space=pltpu.VMEM)
    image = jax.ShapeDtypeStruct((rows, cells), bf16)
    images = pl.pallas_call(
        functools.partial(kernel, parts, groups),
        out_shape=(pltpu.VMEM((rows, cells), bf16), pltpu.VMEM((rows, cells), bf16)),
        in_specs=[pl.BlockSpec(memory_space=pltpu.HBM)] * 6,
        out_specs=(vmem, vmem),
        scratch_shapes=[
            pltpu.VMEM((1, cells), jnp.float32),
            pltpu.VMEM(coupling.shape, bf16),
            pltpu.VMEM(trans.shape, jnp.float32),
            pltpu.VMEM(face_cells.shape, jnp.int32),
            pltpu.VMEM(send_list.shape, jnp.int32),
            pltpu.VMEM((coupling.shape[0], 2 * rows, groups * rows), bf16),
            pltpu.VMEM((coupling.shape[0], groups * rows, 2 * rows), bf16),
            pltpu.VMEM((cells, ghosts + face_count), bf16),
            pltpu.VMEM((face_count + ghosts, cells), bf16),
            pltpu.VMEM((ghosts, face_count), bf16),
            pltpu.VMEM((48, face_count), bf16),
            pltpu.VMEM((2, chunks, groups * rows, BLOCK), bf16),
            pltpu.VMEM((2 * rows, face_count), jnp.float32),
            pltpu.VMEM((groups * rows, face_count), bf16),
            pltpu.VMEM((rows, cells), jnp.float32),
            pltpu.VMEM((2 * rows, face_count), bf16),
            pltpu.VMEM((2, 2, lists, rows, width), bf16),
            pltpu.VMEM((2, 2, lists, rows, width), bf16),
            pltpu.VMEM((lists, 16, width), jnp.float32),
            pltpu.VMEM((lists, 16, width), jnp.float32),
            pltpu.VMEM((8, ghosts), jnp.int32),
            pltpu.VMEM((2 * rows, ghosts), bf16),
            pltpu.SemaphoreType.DMA((chunks + 6,)),
        ]
        + [pltpu.SemaphoreType.DMA((2, chunks))] * 6
        + [pltpu.SemaphoreType.DMA((2, 2, lists))] * 2
        + [pltpu.SemaphoreType.DMA((lists,))] * 2
        + [pltpu.SemaphoreType.DMA((1,))] * 2,
        compiler_params=pltpu.CompilerParams(
            collective_id=0, has_side_effects=True, vmem_limit_bytes=61 * 1024 * 1024
        ),
    )(pressure, storage.reshape(1, cells), coupling, trans, face_cells, send_list)
    hbm = pl.BlockSpec(memory_space=pltpu.HBM)
    return pl.pallas_call(
        write_out,
        out_shape=(image, image),
        in_specs=[vmem] * 2,
        out_specs=(hbm, hbm),
        scratch_shapes=[pltpu.SemaphoreType.DMA((2,))],
        compiler_params=pltpu.CompilerParams(vmem_limit_bytes=1024 * 1024),
    )(*images)


def solution(mesh):
    placed = (
        P("modes", "cells"),
        P("cells"),
        P(None, "modes", None),
        P(None, "cells"),
        P(None, "cells"),
        P("cells", None, None),
    )
    return jax.shard_map(
        functools.partial(local, mesh.shape["cells"], mesh.shape["modes"]),
        mesh=mesh,
        in_specs=placed,
        out_specs=(P("modes", "cells"), P("modes", "cells")),
        check_vma=False,
    )
```

```python
import functools

import jax
import jax.numpy as jnp
from jax import lax
from jax.experimental import pallas as pl
from jax.experimental.pallas import tpu as pltpu
from jax.sharding import PartitionSpec as P

MESH = pl.DeviceIdType.MESH
BLOCK = 256
TILE = 512
AHEAD = 1


def onehot(rows, base, index_row, dtype=jnp.bfloat16):
    near = jnp.clip(index_row - base, -1, rows).astype(jnp.float32).astype(jnp.bfloat16)
    iota = lax.broadcasted_iota(jnp.int32, (rows, index_row.shape[1]), 0)
    return iota.astype(jnp.float32).astype(jnp.bfloat16) == near


def kernel(
    parts, groups, pressure, storage_in, coupling_in, trans_in, faces_in, sends_in, first, second,
    storage, coupling, trans, faces, sends, pair, turned,
    wide, tall, ghost_hot, picked_rows, fields, sums, diff, totals, flux, out_w, in_w, slot_weights, slot_owner, fluxes, out_f,
    out_s, in_s, out_t, in_t,
    load, near_send, near_recv, far_send, far_recv, pass_send, pass_recv,
    w_send, w_recv, f_send, f_recv, pair_send, pair_recv, s_send, s_recv,
    t_send, t_recv,
):
    rows, cells = pressure.shape
    terms = coupling.shape[0]
    face_count = faces.shape[1]
    lists, width = sends.shape[1:]
    ghosts = lists * width
    reach = lists // 2
    offsets = list(range(-reach, 0)) + list(range(1, reach + 1))
    chunks = cells // BLOCK
    part = lax.axis_index("cells")
    group = lax.axis_index("modes")
    partner = group + 1 - 2 * lax.rem(group, 2)
    far = lax.rem(group + 2, 4)
    far_partner = lax.rem(partner + 2, 4)

    def band(member):
        return pl.ds(pl.multiple_of(member * rows, rows), rows)

    mine = band(group)
    one = jnp.ones((), jnp.bfloat16)
    zero = jnp.zeros((), jnp.bfloat16)

    def present(slot):
        return jnp.logical_and(part + offsets[slot] >= 0, part + offsets[slot] < parts)

    def band_copy(app, chunk, member, send_sem, recv_sem, target):
        return pltpu.make_async_remote_copy(
            src_ref=fields.at[app, chunk, band(member)],
            dst_ref=fields.at[app, chunk, band(member)],
            send_sem=send_sem.at[app, chunk],
            recv_sem=recv_sem.at[app, chunk],
            device_id={"modes": target},
            device_id_type=MESH,
        )

    def near_copy(app, chunk, member=group):
        return band_copy(app, chunk, member, near_send, near_recv, partner)

    def far_copy(app, chunk, member=group):
        return band_copy(app, chunk, member, far_send, far_recv, far)

    def pass_copy(app, chunk, member=far):
        return band_copy(app, chunk, member, pass_send, pass_recv, partner)

    def ghost_peer(side, slot):
        peer = part + offsets[slot]
        return {"cells": peer} if side == 0 else {"cells": peer, "modes": partner}

    def half_of(member):
        return pl.ds(pl.multiple_of(lax.rem(member, 2) * rows, rows), rows)

    def ghost_copy(side, slot):
        return pltpu.make_async_remote_copy(
            src_ref=out_w.at[slot],
            dst_ref=in_w.at[lists - 1 - slot, half_of(group)],
            send_sem=w_send.at[side, slot],
            recv_sem=w_recv.at[side, lists - 1 - slot],
            device_id=ghost_peer(side, slot),
            device_id_type=MESH,
        )

    def ghost_wait(side, slot):
        return pltpu.make_async_remote_copy(
            src_ref=out_w.at[lists - 1 - slot],
            dst_ref=in_w.at[slot, half_of(group if side == 0 else partner)],
            send_sem=w_send.at[side, lists - 1 - slot],
            recv_sem=w_recv.at[side, slot],
            device_id=ghost_peer(side, slot),
            device_id_type=MESH,
        )

    def flux_copy():
        return pltpu.make_async_remote_copy(
            src_ref=out_f,
            dst_ref=fluxes.at[rows:2 * rows],
            send_sem=f_send.at[0],
            recv_sem=f_recv.at[0],
            device_id={"modes": far},
            device_id_type=MESH,
        )

    def flux_peer(side, slot):
        peer = part + offsets[slot]
        return {"cells": peer} if side == 0 else {"cells": peer, "modes": far}

    def sum_copy(side, slot):
        return pltpu.make_async_remote_copy(
            src_ref=out_s.at[side, slot],
            dst_ref=in_s.at[side, lists - 1 - slot],
            send_sem=s_send.at[side, slot],
            recv_sem=s_recv.at[side, lists - 1 - slot],
            device_id=flux_peer(side, slot),
            device_id_type=MESH,
        )

    def sum_wait(side, slot):
        return pltpu.make_async_remote_copy(
            src_ref=out_s.at[side, lists - 1 - slot],
            dst_ref=in_s.at[side, slot],
            send_sem=s_send.at[side, lists - 1 - slot],
            recv_sem=s_recv.at[side, slot],
            device_id=flux_peer(side, slot),
            device_id_type=MESH,
        )

    def weight_copy(slot):
        return pltpu.make_async_remote_copy(
            src_ref=out_t.at[slot],
            dst_ref=in_t.at[lists - 1 - slot],
            send_sem=t_send.at[slot],
            recv_sem=t_recv.at[lists - 1 - slot],
            device_id={"cells": part + offsets[slot]},
            device_id_type=MESH,
        )

    def weight_wait(slot):
        return pltpu.make_async_remote_copy(
            src_ref=out_t.at[lists - 1 - slot],
            dst_ref=in_t.at[slot],
            send_sem=t_send.at[lists - 1 - slot],
            recv_sem=t_recv.at[slot],
            device_id={"cells": part + offsets[slot]},
            device_id_type=MESH,
        )

    def pair_copy(member):
        return pltpu.make_async_remote_copy(
            src_ref=pair.at[:, half_of(member)],
            dst_ref=pair.at[:, half_of(member)],
            send_sem=pair_send.at[0],
            recv_sem=pair_recv.at[0],
            device_id={"modes": partner},
            device_id_type=MESH,
        )

    def weight_copy(slot):
        return pltpu.make_async_remote_copy(
            src_ref=out_t.at[slot],
            dst_ref=in_t.at[lists - 1 - slot],
            send_sem=t_send.at[slot],
            recv_sem=t_recv.at[lists - 1 - slot],
            device_id={"cells": part + offsets[slot]},
            device_id_type=MESH,
        )

    def weight_wait(slot):
        return pltpu.make_async_remote_copy(
            src_ref=out_t.at[lists - 1 - slot],
            dst_ref=in_t.at[slot],
            send_sem=t_send.at[lists - 1 - slot],
            recv_sem=t_recv.at[slot],
            device_id={"cells": part + offsets[slot]},
            device_id_type=MESH,
        )

    loads = []
    for index, (source, target) in enumerate(
        [(faces_in, faces), (trans_in, trans), (sends_in, sends)]
        + [
            (pressure.at[:, chunk * BLOCK:(chunk + 1) * BLOCK], fields.at[0, chunk, mine])
            for chunk in range(chunks)
        ]
        + [(coupling_in, pair.at[:, half_of(group)]), (coupling_in, coupling), (storage_in, storage)]
    ):
        loads.append(pltpu.make_async_copy(source, target, load.at[index]))
    for copy in loads:
        copy.start()
    in_w[...] = jnp.zeros_like(in_w)
    in_s[...] = jnp.zeros_like(in_s)
    in_t[...] = jnp.zeros_like(in_t)
    barrier = pltpu.get_barrier_semaphore()
    for peer in (partner, far):
        pl.semaphore_signal(barrier, inc=1, device_id={"modes": peer}, device_id_type=MESH)
    peers = 2
    for slot in range(lists):
        peers = peers + 3 * present(slot).astype(jnp.int32)

        @pl.when(present(slot))
        def _():
            pl.semaphore_signal(
                barrier, inc=1, device_id={"cells": part + offsets[slot]}, device_id_type=MESH
            )
            for peer in (partner, far):
                pl.semaphore_signal(
                    barrier, inc=1, device_id={"cells": part + offsets[slot], "modes": peer}, device_id_type=MESH
                )
    def build_sends(base):
        for slot in range(lists):
            hot = onehot(BLOCK, base, sends[0, slot:slot + 1])
            wide[base:base + BLOCK, slot * width:(slot + 1) * width] = jnp.where(hot, one, zero)

    half = 2 * rows
    near_half = pl.ds(pl.multiple_of(lax.div(group, 2) * half, half), half)
    far_half = pl.ds(pl.multiple_of((1 - lax.div(group, 2)) * half, half), half)

    def build_faces(index, carry):
        at = pl.ds(pl.multiple_of(index * TILE, TILE), TILE)
        to = pl.ds(pl.multiple_of(ghosts + index * TILE, TILE), TILE)
        for chunk in range(chunks):
            base = chunk * BLOCK
            plus = onehot(BLOCK, base, faces[0:1, at])
            minus = onehot(BLOCK, base, faces[1:2, at])
            signs = jnp.where(plus, one, jnp.where(minus, -one, zero))
            wide[base:base + BLOCK, to] = signs
            tall[at, base:base + BLOCK] = signs.T
            part_sum = jnp.dot(fields[0, chunk, near_half], signs, preferred_element_type=jnp.float32)
            total = part_sum if chunk == 0 else total + part_sum
        diff[near_half, at] = total.astype(jnp.bfloat16)
        return carry

    def build_ghost(index, carry):
        at = pl.ds(pl.multiple_of(index * TILE, TILE), TILE)
        other = faces[1:2, at]
        for base in range(0, ghosts, BLOCK):
            hot = onehot(BLOCK, cells + base, other)
            ghost_hot[base:base + BLOCK, at] = jnp.where(hot, one, zero)
        return carry

    def find_slots():
        t = trans[...]
        t_high = t.astype(jnp.bfloat16)
        t_low = (t - t_high.astype(jnp.float32)).astype(jnp.bfloat16)
        picked_rows[...] = jnp.zeros_like(picked_rows)
        picked_rows[0:terms] = t_high
        picked_rows[16:16 + terms] = t_low
        owner_next = faces[0:1] + 1
        picked_rows[32:33] = (owner_next // 32).astype(jnp.float32).astype(jnp.bfloat16)
        picked_rows[33:34] = (owner_next % 32).astype(jnp.float32).astype(jnp.bfloat16)
        lax.fori_loop(0, face_count // TILE, build_ghost, 0)
        found = lax.dot_general(
            picked_rows[...], ghost_hot[...], (((1,), (1,)), ((), ())), preferred_element_type=jnp.float32
        )
        slot_weights[...] = found[0:16] + found[16:32]
        slot_owner[0:1] = (found[32:33] * 32.0 + found[33:34] - 1.0).astype(jnp.int32)
        for slot in range(lists):
            out_t[slot] = slot_weights[:, slot * width:(slot + 1) * width]

    def build_owners():
        for base in range(0, cells, BLOCK):
            hot = onehot(BLOCK, base, slot_owner[0:1])
            tall[face_count:, base:base + BLOCK] = jnp.where(hot, -one, zero).T

    def differ(app, chunk, members):
        rows_of = slice(chunk * BLOCK, (chunk + 1) * BLOCK)
        field = fields[app, chunk, members]
        for start in range(0, face_count, TILE):
            at = slice(start, start + TILE)
            total = jnp.dot(
                field, wide[rows_of, ghosts + start:ghosts + start + TILE], preferred_element_type=jnp.float32
            )
            if chunk > 0:
                total += sums[:, at]
            if chunk < chunks - 1:
                sums[:, at] = total
            else:
                diff[members, at] = total.astype(jnp.bfloat16)

    def pick(app, members):
        total = jnp.dot(fields[app, 0, members], wide[0:BLOCK, 0:ghosts], preferred_element_type=jnp.float32)
        for chunk in range(1, chunks):
            total += jnp.dot(
                fields[app, chunk, members], wide[chunk * BLOCK:(chunk + 1) * BLOCK, 0:ghosts],
                preferred_element_type=jnp.float32,
            )
        return total.astype(jnp.bfloat16)

    def send_ghosts():
        total = pick(0, mine)
        for slot in range(lists):
            out_w[slot] = total[:, slot * width:(slot + 1) * width]

            @pl.when(present(slot))
            def _():
                for side in range(2):
                    ghost_copy(side, slot).start()

    def send_sums():
        ghost = pick(1, near_half)
        for slot in range(lists):
            @pl.when(present(slot))
            def _():
                weight_wait(slot).wait_recv()
        weights = jnp.concatenate([in_t[slot] for slot in range(lists)], axis=1)
        for side, member in ((1, far), (0, group)):
            sent = mix(turned[:, band(member)].reshape(terms * rows, half), ghost, weights)
            for slot in range(lists):
                out_s[side, slot] = sent[:, slot * width:(slot + 1) * width].astype(jnp.bfloat16)

                @pl.when(present(slot))
                def _():
                    sum_copy(side, slot).start()

    def mix_ghosts():
        for slot in range(lists):
            @pl.when(present(slot))
            def _():
                for side in range(2):
                    ghost_wait(side, slot).wait_recv()
        ghost = jnp.concatenate([in_w[slot] for slot in range(lists)], axis=1)
        for member in (far, group):
            sent = mix(turned[:, band(member)].reshape(terms * rows, half), ghost, slot_weights[...])
            if member is far:
                out_f[...] = sent.astype(jnp.bfloat16)
                flux_copy().start()
            else:
                fluxes[0:rows] = sent.astype(jnp.bfloat16)

    def pass_on(app, chunk):
        far_copy(app, chunk, far).wait_recv()
        pass_copy(app, chunk).start()

    def mix(stacked, column, weights):
        mixed = jnp.dot(stacked, column, preferred_element_type=jnp.float32)
        total = mixed[0:rows] * weights[0:1]
        for term in range(1, terms):
            total += mixed[term * rows:(term + 1) * rows] * weights[term:term + 1]
        return total

    for copy in loads[:3]:
        copy.wait()
    find_slots()
    for chunk in range(chunks):
        build_sends(chunk * BLOCK)
    for copy in loads[3:]:
        copy.wait()
    pl.semaphore_wait(barrier, peers)
    for chunk in range(chunks):
        far_copy(0, chunk).start()
        near_copy(0, chunk).start()
    send_ghosts()
    pair_copy(group).start()
    for slot in range(lists):
        @pl.when(present(slot))
        def _():
            weight_copy(slot).start()
    for chunk in range(chunks):
        near_copy(0, chunk, partner).wait_recv()
    lax.fori_loop(0, face_count // TILE, build_faces, 0)
    pair_copy(partner).wait_recv()
    for term in range(terms):
        turned[term] = pair[term].T
    for app, target in enumerate((first, second)):
        if app == 1:
            for chunk in range(chunks):
                near_copy(app, chunk, partner).wait_recv()
            send_sums()
        for chunk in range(chunks):
            pass_on(app, chunk)
            if app == 1:
                differ(app, chunk, near_half)
        if app == 0:
            mix_ghosts()
            build_owners()
        for chunk in range(chunks):
            pass_copy(app, chunk, far_partner).wait_recv()
            differ(app, chunk, far_half)

        stacked = coupling[...].reshape(terms * rows, groups * rows)
        for start in range(0, face_count, TILE):
            at = slice(start, start + TILE)
            total = mix(stacked, diff[:, at], trans[:, at])
            high = total.astype(jnp.bfloat16)
            flux[0:rows, at] = high
            flux[rows:2 * rows, at] = (total - high.astype(jnp.float32)).astype(jnp.bfloat16)

        def inner(chunk):
            span = slice(chunk * BLOCK, (chunk + 1) * BLOCK)
            spread = jnp.dot(flux[...], tall[0:face_count, span], preferred_element_type=jnp.float32)
            image = storage[:, span] * fields[app, chunk, mine, :].astype(jnp.float32)
            totals[:, span] = image + spread[0:rows] + spread[rows:2 * rows]

        def finish(chunk):
            span = slice(chunk * BLOCK, (chunk + 1) * BLOCK)
            spread = jnp.dot(arrived, tall[face_count:, span], preferred_element_type=jnp.float32)
            image = (totals[:, span] + (spread[0:rows] + spread[rows:half])).astype(jnp.bfloat16)
            target[:, span] = image
            if app == 0:
                fields[1, chunk, mine, :] = image
                far_copy(1, chunk).start()
                near_copy(1, chunk).start()

        for chunk in range(AHEAD):
            inner(chunk)
        if app == 0:
            flux_copy().wait_recv()
            arrived = fluxes[...]
        else:
            for slot in range(lists):
                @pl.when(present(slot))
                def _():
                    for side in range(2):
                        sum_wait(side, slot).wait_recv()
            arrived = jnp.concatenate(
                [jnp.concatenate([in_s[side, slot] for slot in range(lists)], axis=1) for side in range(2)], axis=0
            )
        for chunk in range(chunks):
            if chunk >= AHEAD:
                inner(chunk)
            finish(chunk)

    for app in range(2):
        for chunk in range(chunks):
            far_copy(app, chunk).wait_send()
            near_copy(app, chunk).wait_send()
            pass_copy(app, chunk).wait_send()
    flux_copy().wait_send()
    for slot in range(lists):
        @pl.when(present(slot))
        def _():
            weight_copy(slot).wait_send()
            for side in range(2):
                ghost_copy(side, slot).wait_send()
                sum_copy(side, slot).wait_send()
    pair_copy(group).wait_send()


def write_out(first_in, second_in, first, second, done):
    copies = [
        pltpu.make_async_copy(source, target, done.at[index])
        for index, (source, target) in enumerate(((first_in, first), (second_in, second)))
    ]
    for copy in copies:
        copy.start()
    for copy in copies:
        copy.wait()


def local(parts, groups, pressure, storage, coupling, trans, face_cells, send_list):
    assert groups == 4
    rows, cells = pressure.shape
    face_count = face_cells.shape[1]
    lists, width = send_list.shape[1:]
    ghosts = lists * width
    chunks = cells // BLOCK
    bf16 = jnp.bfloat16
    vmem = pl.BlockSpec(memory_space=pltpu.VMEM)
    image = jax.ShapeDtypeStruct((rows, cells), bf16)
    images = pl.pallas_call(
        functools.partial(kernel, parts, groups),
        out_shape=(pltpu.VMEM((rows, cells), bf16), pltpu.VMEM((rows, cells), bf16)),
        in_specs=[pl.BlockSpec(memory_space=pltpu.HBM)] * 6,
        out_specs=(vmem, vmem),
        scratch_shapes=[
            pltpu.VMEM((1, cells), jnp.float32),
            pltpu.VMEM(coupling.shape, bf16),
            pltpu.VMEM(trans.shape, jnp.float32),
            pltpu.VMEM(face_cells.shape, jnp.int32),
            pltpu.VMEM(send_list.shape, jnp.int32),
            pltpu.VMEM((coupling.shape[0], 2 * rows, groups * rows), bf16),
            pltpu.VMEM((coupling.shape[0], groups * rows, 2 * rows), bf16),
            pltpu.VMEM((cells, ghosts + face_count), bf16),
            pltpu.VMEM((face_count + ghosts, cells), bf16),
            pltpu.VMEM((ghosts, face_count), bf16),
            pltpu.VMEM((48, face_count), bf16),
            pltpu.VMEM((2, chunks, groups * rows, BLOCK), bf16),
            pltpu.VMEM((2 * rows, face_count), jnp.float32),
            pltpu.VMEM((groups * rows, face_count), bf16),
            pltpu.VMEM((rows, cells), jnp.float32),
            pltpu.VMEM((2 * rows, face_count), bf16),
            pltpu.VMEM((lists, rows, width), bf16),
            pltpu.VMEM((lists, 2 * rows, width), bf16),
            pltpu.VMEM((16, ghosts), jnp.float32),
            pltpu.VMEM((8, ghosts), jnp.int32),
            pltpu.VMEM((2 * rows, ghosts), bf16),
            pltpu.VMEM((rows, ghosts), bf16),
            pltpu.VMEM((2, lists, rows, width), bf16),
            pltpu.VMEM((2, lists, rows, width), bf16),
            pltpu.VMEM((lists, 16, width), jnp.float32),
            pltpu.VMEM((lists, 16, width), jnp.float32),
            pltpu.SemaphoreType.DMA((chunks + 6,)),
        ]
        + [pltpu.SemaphoreType.DMA((2, chunks))] * 6
        + [pltpu.SemaphoreType.DMA((2, lists))] * 2
        + [pltpu.SemaphoreType.DMA((1,))] * 4
        + [pltpu.SemaphoreType.DMA((2, lists))] * 2
        + [pltpu.SemaphoreType.DMA((lists,))] * 2,
        compiler_params=pltpu.CompilerParams(
            collective_id=0, has_side_effects=True, vmem_limit_bytes=61 * 1024 * 1024
        ),
    )(pressure, storage.reshape(1, cells), coupling, trans, face_cells, send_list)
    hbm = pl.BlockSpec(memory_space=pltpu.HBM)
    return pl.pallas_call(
        write_out,
        out_shape=(image, image),
        in_specs=[vmem] * 2,
        out_specs=(hbm, hbm),
        scratch_shapes=[pltpu.SemaphoreType.DMA((2,))],
        compiler_params=pltpu.CompilerParams(vmem_limit_bytes=1024 * 1024),
    )(*images)


def solution(mesh):
    placed = (
        P("modes", "cells"),
        P("cells"),
        P(None, "modes", None),
        P(None, "cells"),
        P(None, "cells"),
        P("cells", None, None),
    )
    return jax.shard_map(
        functools.partial(local, mesh.shape["cells"], mesh.shape["modes"]),
        mesh=mesh,
        in_specs=placed,
        out_specs=(P("modes", "cells"), P("modes", "cells")),
        check_vma=False,
    )
```

```python
import functools

import jax
import jax.numpy as jnp
from jax import lax
from jax.experimental import pallas as pl
from jax.experimental.pallas import tpu as pltpu
from jax.sharding import PartitionSpec as P

MESH = pl.DeviceIdType.MESH
BLOCK = 256
TILE = 512
AHEAD = 1


def onehot(rows, base, index_row, dtype=jnp.bfloat16):
    near = jnp.clip(index_row - base, -1, rows).astype(jnp.float32).astype(jnp.bfloat16)
    iota = lax.broadcasted_iota(jnp.int32, (rows, index_row.shape[1]), 0)
    return iota.astype(jnp.float32).astype(jnp.bfloat16) == near


def kernel(
    parts, groups, pressure, storage_in, coupling_in, trans_in, faces_in, sends_in, first, second,
    storage, coupling, trans, faces, sends, pair, turned,
    wide, tall, ghost_hot, picked_rows, fields, sums, diff, totals, flux, out_w, in_w, slot_weights, slot_owner, fluxes, out_f,
    out_s, in_s, out_t, in_t,
    load, near_send, near_recv, far_send, far_recv, pass_send, pass_recv,
    w_send, w_recv, f_send, f_recv, pair_send, pair_recv, s_send, s_recv,
    t_send, t_recv,
):
    rows, cells = pressure.shape
    terms = coupling.shape[0]
    face_count = faces.shape[1]
    lists, width = sends.shape[1:]
    ghosts = lists * width
    reach = lists // 2
    offsets = list(range(-reach, 0)) + list(range(1, reach + 1))
    chunks = cells // BLOCK
    part = lax.axis_index("cells")
    group = lax.axis_index("modes")
    partner = group + 1 - 2 * lax.rem(group, 2)
    far = lax.rem(group + 2, 4)
    far_partner = lax.rem(partner + 2, 4)

    def band(member):
        return pl.ds(pl.multiple_of(member * rows, rows), rows)

    mine = band(group)
    one = jnp.ones((), jnp.bfloat16)
    zero = jnp.zeros((), jnp.bfloat16)

    def present(slot):
        return jnp.logical_and(part + offsets[slot] >= 0, part + offsets[slot] < parts)

    def band_copy(app, chunk, member, send_sem, recv_sem, target):
        return pltpu.make_async_remote_copy(
            src_ref=fields.at[app, chunk, band(member)],
            dst_ref=fields.at[app, chunk, band(member)],
            send_sem=send_sem.at[app, chunk],
            recv_sem=recv_sem.at[app, chunk],
            device_id={"modes": target},
            device_id_type=MESH,
        )

    def near_copy(app, chunk, member=group):
        return band_copy(app, chunk, member, near_send, near_recv, partner)

    def far_copy(app, chunk, member=group):
        return band_copy(app, chunk, member, far_send, far_recv, far)

    def pass_copy(app, chunk, member=far):
        return band_copy(app, chunk, member, pass_send, pass_recv, partner)

    def ghost_peer(side, slot):
        peer = part + offsets[slot]
        return {"cells": peer} if side == 0 else {"cells": peer, "modes": partner}

    def half_of(member):
        return pl.ds(pl.multiple_of(lax.rem(member, 2) * rows, rows), rows)

    def ghost_copy(side, slot):
        return pltpu.make_async_remote_copy(
            src_ref=out_w.at[slot],
            dst_ref=in_w.at[lists - 1 - slot, half_of(group)],
            send_sem=w_send.at[side, slot],
            recv_sem=w_recv.at[side, lists - 1 - slot],
            device_id=ghost_peer(side, slot),
            device_id_type=MESH,
        )

    def ghost_wait(side, slot):
        return pltpu.make_async_remote_copy(
            src_ref=out_w.at[lists - 1 - slot],
            dst_ref=in_w.at[slot, half_of(group if side == 0 else partner)],
            send_sem=w_send.at[side, lists - 1 - slot],
            recv_sem=w_recv.at[side, slot],
            device_id=ghost_peer(side, slot),
            device_id_type=MESH,
        )

    def flux_copy():
        return pltpu.make_async_remote_copy(
            src_ref=out_f,
            dst_ref=fluxes.at[rows:2 * rows],
            send_sem=f_send.at[0],
            recv_sem=f_recv.at[0],
            device_id={"modes": far},
            device_id_type=MESH,
        )

    def flux_peer(side, slot):
        peer = part + offsets[slot]
        return {"cells": peer} if side == 0 else {"cells": peer, "modes": far}

    def sum_copy(side, slot):
        return pltpu.make_async_remote_copy(
            src_ref=out_s.at[side, slot],
            dst_ref=in_s.at[side, lists - 1 - slot],
            send_sem=s_send.at[side, slot],
            recv_sem=s_recv.at[side, lists - 1 - slot],
            device_id=flux_peer(side, slot),
            device_id_type=MESH,
        )

    def sum_wait(side, slot):
        return pltpu.make_async_remote_copy(
            src_ref=out_s.at[side, lists - 1 - slot],
            dst_ref=in_s.at[side, slot],
            send_sem=s_send.at[side, lists - 1 - slot],
            recv_sem=s_recv.at[side, slot],
            device_id=flux_peer(side, slot),
            device_id_type=MESH,
        )

    def weight_copy(slot):
        return pltpu.make_async_remote_copy(
            src_ref=out_t.at[slot],
            dst_ref=in_t.at[lists - 1 - slot],
            send_sem=t_send.at[slot],
            recv_sem=t_recv.at[lists - 1 - slot],
            device_id={"cells": part + offsets[slot]},
            device_id_type=MESH,
        )

    def weight_wait(slot):
        return pltpu.make_async_remote_copy(
            src_ref=out_t.at[lists - 1 - slot],
            dst_ref=in_t.at[slot],
            send_sem=t_send.at[lists - 1 - slot],
            recv_sem=t_recv.at[slot],
            device_id={"cells": part + offsets[slot]},
            device_id_type=MESH,
        )

    def pair_copy(member):
        return pltpu.make_async_remote_copy(
            src_ref=pair.at[:, half_of(member)],
            dst_ref=pair.at[:, half_of(member)],
            send_sem=pair_send.at[0],
            recv_sem=pair_recv.at[0],
            device_id={"modes": partner},
            device_id_type=MESH,
        )

    def weight_copy(slot):
        return pltpu.make_async_remote_copy(
            src_ref=out_t.at[slot],
            dst_ref=in_t.at[lists - 1 - slot],
            send_sem=t_send.at[slot],
            recv_sem=t_recv.at[lists - 1 - slot],
            device_id={"cells": part + offsets[slot]},
            device_id_type=MESH,
        )

    def weight_wait(slot):
        return pltpu.make_async_remote_copy(
            src_ref=out_t.at[lists - 1 - slot],
            dst_ref=in_t.at[slot],
            send_sem=t_send.at[lists - 1 - slot],
            recv_sem=t_recv.at[slot],
            device_id={"cells": part + offsets[slot]},
            device_id_type=MESH,
        )

    loads = []
    for index, (source, target) in enumerate(
        [(faces_in, faces), (trans_in, trans), (sends_in, sends)]
        + [
            (pressure.at[:, chunk * BLOCK:(chunk + 1) * BLOCK], fields.at[0, chunk, mine])
            for chunk in range(chunks)
        ]
        + [(coupling_in, pair.at[:, half_of(group)]), (coupling_in, coupling), (storage_in, storage)]
    ):
        loads.append(pltpu.make_async_copy(source, target, load.at[index]))
    for copy in loads:
        copy.start()
    in_w[...] = jnp.zeros_like(in_w)
    in_s[...] = jnp.zeros_like(in_s)
    in_t[...] = jnp.zeros_like(in_t)
    barrier = pltpu.get_barrier_semaphore()
    for peer in (partner, far):
        pl.semaphore_signal(barrier, inc=1, device_id={"modes": peer}, device_id_type=MESH)
    peers = 2
    for slot in range(lists):
        peers = peers + 3 * present(slot).astype(jnp.int32)

        @pl.when(present(slot))
        def _():
            pl.semaphore_signal(
                barrier, inc=1, device_id={"cells": part + offsets[slot]}, device_id_type=MESH
            )
            for peer in (partner, far):
                pl.semaphore_signal(
                    barrier, inc=1, device_id={"cells": part + offsets[slot], "modes": peer}, device_id_type=MESH
                )
    def build_sends(base):
        for slot in range(lists):
            hot = onehot(BLOCK, base, sends[0, slot:slot + 1])
            wide[base:base + BLOCK, slot * width:(slot + 1) * width] = jnp.where(hot, one, zero)

    half = 2 * rows
    near_half = pl.ds(pl.multiple_of(lax.div(group, 2) * half, half), half)
    far_half = pl.ds(pl.multiple_of((1 - lax.div(group, 2)) * half, half), half)

    def build_faces(index, carry):
        at = pl.ds(pl.multiple_of(index * TILE, TILE), TILE)
        to = pl.ds(pl.multiple_of(ghosts + index * TILE, TILE), TILE)
        for chunk in range(chunks):
            base = chunk * BLOCK
            plus = onehot(BLOCK, base, faces[0:1, at])
            minus = onehot(BLOCK, base, faces[1:2, at])
            signs = jnp.where(plus, one, jnp.where(minus, -one, zero))
            wide[base:base + BLOCK, to] = signs
            tall[at, base:base + BLOCK] = signs.T
            part_sum = jnp.dot(fields[0, chunk, near_half], signs, preferred_element_type=jnp.float32)
            total = part_sum if chunk == 0 else total + part_sum
        diff[near_half, at] = total.astype(jnp.bfloat16)
        return carry

    def build_ghost(index, carry):
        at = pl.ds(pl.multiple_of(index * TILE, TILE), TILE)
        other = faces[1:2, at]
        for base in range(0, ghosts, BLOCK):
            hot = onehot(BLOCK, cells + base, other)
            ghost_hot[base:base + BLOCK, at] = jnp.where(hot, one, zero)
        return carry

    def find_slots():
        t = trans[...]
        t_high = t.astype(jnp.bfloat16)
        t_low = (t - t_high.astype(jnp.float32)).astype(jnp.bfloat16)
        picked_rows[...] = jnp.zeros_like(picked_rows)
        picked_rows[0:terms] = t_high
        picked_rows[16:16 + terms] = t_low
        owner_next = faces[0:1] + 1
        picked_rows[32:33] = (owner_next // 32).astype(jnp.float32).astype(jnp.bfloat16)
        picked_rows[33:34] = (owner_next % 32).astype(jnp.float32).astype(jnp.bfloat16)
        lax.fori_loop(0, face_count // TILE, build_ghost, 0)

    def weigh_slots():
        found = lax.dot_general(
            picked_rows[...], ghost_hot[...], (((1,), (1,)), ((), ())), preferred_element_type=jnp.float32
        )
        slot_weights[...] = found[0:16] + found[16:32]
        slot_owner[0:1] = (found[32:33] * 32.0 + found[33:34] - 1.0).astype(jnp.int32)
        for slot in range(lists):
            out_t[slot] = slot_weights[:, slot * width:(slot + 1) * width]

    def build_owners():
        for base in range(0, cells, BLOCK):
            hot = onehot(BLOCK, base, slot_owner[0:1])
            tall[face_count:, base:base + BLOCK] = jnp.where(hot, -one, zero).T

    def differ(app, chunk, members):
        rows_of = slice(chunk * BLOCK, (chunk + 1) * BLOCK)
        field = fields[app, chunk, members]
        for start in range(0, face_count, TILE):
            at = slice(start, start + TILE)
            total = jnp.dot(
                field, wide[rows_of, ghosts + start:ghosts + start + TILE], preferred_element_type=jnp.float32
            )
            if chunk > 0:
                total += sums[:, at]
            if chunk < chunks - 1:
                sums[:, at] = total
            else:
                diff[members, at] = total.astype(jnp.bfloat16)

    def pick(app, members):
        total = jnp.dot(fields[app, 0, members], wide[0:BLOCK, 0:ghosts], preferred_element_type=jnp.float32)
        for chunk in range(1, chunks):
            total += jnp.dot(
                fields[app, chunk, members], wide[chunk * BLOCK:(chunk + 1) * BLOCK, 0:ghosts],
                preferred_element_type=jnp.float32,
            )
        return total.astype(jnp.bfloat16)

    def send_ghosts():
        total = pick(0, mine)
        for slot in range(lists):
            out_w[slot] = total[:, slot * width:(slot + 1) * width]

            @pl.when(present(slot))
            def _():
                for side in range(2):
                    ghost_copy(side, slot).start()

    def send_sums():
        ghost = pick(1, near_half)
        for slot in range(lists):
            @pl.when(present(slot))
            def _():
                weight_wait(slot).wait_recv()
        weights = jnp.concatenate([in_t[slot] for slot in range(lists)], axis=1)
        for side, member in ((1, far), (0, group)):
            sent = mix(turned[:, band(member)].reshape(terms * rows, half), ghost, weights)
            for slot in range(lists):
                out_s[side, slot] = sent[:, slot * width:(slot + 1) * width].astype(jnp.bfloat16)

                @pl.when(present(slot))
                def _():
                    sum_copy(side, slot).start()

    def mix_ghosts():
        for slot in range(lists):
            @pl.when(present(slot))
            def _():
                for side in range(2):
                    ghost_wait(side, slot).wait_recv()
        ghost = jnp.concatenate([in_w[slot] for slot in range(lists)], axis=1)
        for member in (far, group):
            sent = mix(turned[:, band(member)].reshape(terms * rows, half), ghost, slot_weights[...])
            if member is far:
                out_f[...] = sent.astype(jnp.bfloat16)
                flux_copy().start()
            else:
                fluxes[0:rows] = sent.astype(jnp.bfloat16)

    def pass_on(app, chunk):
        far_copy(app, chunk, far).wait_recv()
        pass_copy(app, chunk).start()

    def mix(stacked, column, weights):
        mixed = jnp.dot(stacked, column, preferred_element_type=jnp.float32)
        total = mixed[0:rows] * weights[0:1]
        for term in range(1, terms):
            total += mixed[term * rows:(term + 1) * rows] * weights[term:term + 1]
        return total

    for copy in loads[:3]:
        copy.wait()
    find_slots()
    for copy in loads[3:]:
        copy.wait()
    pl.semaphore_wait(barrier, peers)
    for chunk in range(chunks):
        far_copy(0, chunk).start()
        near_copy(0, chunk).start()
    pair_copy(group).start()
    for chunk in range(chunks):
        build_sends(chunk * BLOCK)
    send_ghosts()
    for chunk in range(chunks):
        near_copy(0, chunk, partner).wait_recv()
    lax.fori_loop(0, face_count // TILE, build_faces, 0, unroll=True)
    pair_copy(partner).wait_recv()
    for term in range(terms):
        turned[term] = pair[term].T
    weigh_slots()
    for slot in range(lists):
        @pl.when(present(slot))
        def _():
            weight_copy(slot).start()
    for app, target in enumerate((first, second)):
        if app == 1:
            for chunk in range(chunks):
                near_copy(app, chunk, partner).wait_recv()
            send_sums()
        for chunk in range(chunks):
            pass_on(app, chunk)
            if app == 1:
                differ(app, chunk, near_half)
        if app == 0:
            mix_ghosts()
            build_owners()
        for chunk in range(chunks):
            pass_copy(app, chunk, far_partner).wait_recv()
            differ(app, chunk, far_half)

        stacked = coupling[...].reshape(terms * rows, groups * rows)
        for start in range(0, face_count, TILE):
            at = slice(start, start + TILE)
            total = mix(stacked, diff[:, at], trans[:, at])
            high = total.astype(jnp.bfloat16)
            flux[0:rows, at] = high
            flux[rows:2 * rows, at] = (total - high.astype(jnp.float32)).astype(jnp.bfloat16)

        def inner(chunk):
            span = slice(chunk * BLOCK, (chunk + 2) * BLOCK)
            spread = jnp.dot(flux[...], tall[0:face_count, span], preferred_element_type=jnp.float32)
            own = jnp.concatenate([fields[app, chunk, mine], fields[app, chunk + 1, mine]], axis=1)
            image = storage[:, span] * own.astype(jnp.float32)
            totals[:, span] = image + spread[0:rows] + spread[rows:2 * rows]

        def finish(chunk):
            span = slice(chunk * BLOCK, (chunk + 1) * BLOCK)
            spread = jnp.dot(arrived, tall[face_count:, span], preferred_element_type=jnp.float32)
            image = (totals[:, span] + (spread[0:rows] + spread[rows:half])).astype(jnp.bfloat16)
            target[:, span] = image
            if app == 0:
                fields[1, chunk, mine, :] = image
                far_copy(1, chunk).start()
                near_copy(1, chunk).start()

        inner(0)
        if app == 0:
            flux_copy().wait_recv()
            arrived = fluxes[...]
        else:
            for slot in range(lists):
                @pl.when(present(slot))
                def _():
                    for side in range(2):
                        sum_wait(side, slot).wait_recv()
            arrived = jnp.concatenate(
                [jnp.concatenate([in_s[side, slot] for slot in range(lists)], axis=1) for side in range(2)], axis=0
            )
        for chunk in range(chunks):
            if chunk > 0 and chunk % 2 == 0:
                inner(chunk)
            finish(chunk)

    for app in range(2):
        for chunk in range(chunks):
            far_copy(app, chunk).wait_send()
            near_copy(app, chunk).wait_send()
            pass_copy(app, chunk).wait_send()
    flux_copy().wait_send()
    for slot in range(lists):
        @pl.when(present(slot))
        def _():
            weight_copy(slot).wait_send()
            for side in range(2):
                ghost_copy(side, slot).wait_send()
                sum_copy(side, slot).wait_send()
    pair_copy(group).wait_send()


def write_out(first_in, second_in, first, second, done):
    copies = [
        pltpu.make_async_copy(source, target, done.at[index])
        for index, (source, target) in enumerate(((first_in, first), (second_in, second)))
    ]
    for copy in copies:
        copy.start()
    for copy in copies:
        copy.wait()


def local(parts, groups, pressure, storage, coupling, trans, face_cells, send_list):
    assert groups == 4
    rows, cells = pressure.shape
    face_count = face_cells.shape[1]
    lists, width = send_list.shape[1:]
    ghosts = lists * width
    chunks = cells // BLOCK
    bf16 = jnp.bfloat16
    vmem = pl.BlockSpec(memory_space=pltpu.VMEM)
    image = jax.ShapeDtypeStruct((rows, cells), bf16)
    images = pl.pallas_call(
        functools.partial(kernel, parts, groups),
        out_shape=(pltpu.VMEM((rows, cells), bf16), pltpu.VMEM((rows, cells), bf16)),
        in_specs=[pl.BlockSpec(memory_space=pltpu.HBM)] * 6,
        out_specs=(vmem, vmem),
        scratch_shapes=[
            pltpu.VMEM((1, cells), jnp.float32),
            pltpu.VMEM(coupling.shape, bf16),
            pltpu.VMEM(trans.shape, jnp.float32),
            pltpu.VMEM(face_cells.shape, jnp.int32),
            pltpu.VMEM(send_list.shape, jnp.int32),
            pltpu.VMEM((coupling.shape[0], 2 * rows, groups * rows), bf16),
            pltpu.VMEM((coupling.shape[0], groups * rows, 2 * rows), bf16),
            pltpu.VMEM((cells, ghosts + face_count), bf16),
            pltpu.VMEM((face_count + ghosts, cells), bf16),
            pltpu.VMEM((ghosts, face_count), bf16),
            pltpu.VMEM((48, face_count), bf16),
            pltpu.VMEM((2, chunks, groups * rows, BLOCK), bf16),
            pltpu.VMEM((2 * rows, face_count), jnp.float32),
            pltpu.VMEM((groups * rows, face_count), bf16),
            pltpu.VMEM((rows, cells), jnp.float32),
            pltpu.VMEM((2 * rows, face_count), bf16),
            pltpu.VMEM((lists, rows, width), bf16),
            pltpu.VMEM((lists, 2 * rows, width), bf16),
            pltpu.VMEM((16, ghosts), jnp.float32),
            pltpu.VMEM((8, ghosts), jnp.int32),
            pltpu.VMEM((2 * rows, ghosts), bf16),
            pltpu.VMEM((rows, ghosts), bf16),
            pltpu.VMEM((2, lists, rows, width), bf16),
            pltpu.VMEM((2, lists, rows, width), bf16),
            pltpu.VMEM((lists, 16, width), jnp.float32),
            pltpu.VMEM((lists, 16, width), jnp.float32),
            pltpu.SemaphoreType.DMA((chunks + 6,)),
        ]
        + [pltpu.SemaphoreType.DMA((2, chunks))] * 6
        + [pltpu.SemaphoreType.DMA((2, lists))] * 2
        + [pltpu.SemaphoreType.DMA((1,))] * 4
        + [pltpu.SemaphoreType.DMA((2, lists))] * 2
        + [pltpu.SemaphoreType.DMA((lists,))] * 2,
        compiler_params=pltpu.CompilerParams(
            collective_id=0, has_side_effects=True, vmem_limit_bytes=61 * 1024 * 1024
        ),
    )(pressure, storage.reshape(1, cells), coupling, trans, face_cells, send_list)
    hbm = pl.BlockSpec(memory_space=pltpu.HBM)
    return pl.pallas_call(
        write_out,
        out_shape=(image, image),
        in_specs=[vmem] * 2,
        out_specs=(hbm, hbm),
        scratch_shapes=[pltpu.SemaphoreType.DMA((2,))],
        compiler_params=pltpu.CompilerParams(vmem_limit_bytes=1024 * 1024),
    )(*images)


def solution(mesh):
    placed = (
        P("modes", "cells"),
        P("cells"),
        P(None, "modes", None),
        P(None, "cells"),
        P(None, "cells"),
        P("cells", None, None),
    )
    return jax.shard_map(
        functools.partial(local, mesh.shape["cells"], mesh.shape["modes"]),
        mesh=mesh,
        in_specs=placed,
        out_specs=(P("modes", "cells"), P("modes", "cells")),
        check_vma=False,
    )
```

```python
import functools

import jax
import jax.numpy as jnp
from jax import lax
from jax.experimental import pallas as pl
from jax.experimental.pallas import tpu as pltpu
from jax.sharding import PartitionSpec as P

MESH = pl.DeviceIdType.MESH
BLOCK = 256
TILE = 512
WIDE = 1536


def onehot(rows, base, index_row, dtype=jnp.bfloat16):
    near = jnp.clip(index_row - base, -1, rows).astype(jnp.float32).astype(jnp.bfloat16)
    iota = lax.broadcasted_iota(jnp.int32, (rows, index_row.shape[1]), 0)
    return iota.astype(jnp.float32).astype(jnp.bfloat16) == near


def kernel(
    parts, groups, pressure, storage_in, coupling_in, trans_in, faces_in, sends_in, first, second,
    storage, coupling, trans, faces, sends, pair, turned,
    wide, tall, ghost_hot, picked_rows, fields, sums, diff, totals, flux, out_w, in_w, slot_weights, slot_owner, fluxes, out_f,
    out_s, in_s, out_t, in_t,
    load, near_send, near_recv, far_send, far_recv, pass_send, pass_recv,
    w_send, w_recv, f_send, f_recv, pair_send, pair_recv, s_send, s_recv,
    t_send, t_recv,
):
    rows, cells = pressure.shape
    terms = coupling.shape[0]
    face_count = faces.shape[1]
    lists, width = sends.shape[1:]
    ghosts = lists * width
    reach = lists // 2
    offsets = list(range(-reach, 0)) + list(range(1, reach + 1))
    chunks = cells // BLOCK
    part = lax.axis_index("cells")
    group = lax.axis_index("modes")
    partner = group + 1 - 2 * lax.rem(group, 2)
    far = lax.rem(group + 2, 4)
    far_partner = lax.rem(partner + 2, 4)

    def band(member):
        return pl.ds(pl.multiple_of(member * rows, rows), rows)

    mine = band(group)
    one = jnp.ones((), jnp.bfloat16)
    zero = jnp.zeros((), jnp.bfloat16)

    def present(slot):
        return jnp.logical_and(part + offsets[slot] >= 0, part + offsets[slot] < parts)

    def band_copy(app, chunk, member, send_sem, recv_sem, target):
        return pltpu.make_async_remote_copy(
            src_ref=fields.at[app, chunk, band(member)],
            dst_ref=fields.at[app, chunk, band(member)],
            send_sem=send_sem.at[app, chunk],
            recv_sem=recv_sem.at[app, chunk],
            device_id={"modes": target},
            device_id_type=MESH,
        )

    def near_copy(app, chunk, member=group):
        return band_copy(app, chunk, member, near_send, near_recv, partner)

    def far_copy(app, chunk, member=group):
        return band_copy(app, chunk, member, far_send, far_recv, far)

    def pass_copy(app, chunk, member=far):
        return band_copy(app, chunk, member, pass_send, pass_recv, partner)

    def ghost_peer(side, slot):
        peer = part + offsets[slot]
        return {"cells": peer} if side == 0 else {"cells": peer, "modes": partner}

    def half_of(member):
        return pl.ds(pl.multiple_of(lax.rem(member, 2) * rows, rows), rows)

    def ghost_copy(side, slot):
        return pltpu.make_async_remote_copy(
            src_ref=out_w.at[slot],
            dst_ref=in_w.at[lists - 1 - slot, half_of(group)],
            send_sem=w_send.at[side, slot],
            recv_sem=w_recv.at[side, lists - 1 - slot],
            device_id=ghost_peer(side, slot),
            device_id_type=MESH,
        )

    def ghost_wait(side, slot):
        return pltpu.make_async_remote_copy(
            src_ref=out_w.at[lists - 1 - slot],
            dst_ref=in_w.at[slot, half_of(group if side == 0 else partner)],
            send_sem=w_send.at[side, lists - 1 - slot],
            recv_sem=w_recv.at[side, slot],
            device_id=ghost_peer(side, slot),
            device_id_type=MESH,
        )

    def flux_copy():
        return pltpu.make_async_remote_copy(
            src_ref=out_f,
            dst_ref=fluxes.at[rows:2 * rows],
            send_sem=f_send.at[0],
            recv_sem=f_recv.at[0],
            device_id={"modes": far},
            device_id_type=MESH,
        )

    def flux_peer(side, slot):
        peer = part + offsets[slot]
        return {"cells": peer} if side == 0 else {"cells": peer, "modes": far}

    def sum_copy(side, slot):
        return pltpu.make_async_remote_copy(
            src_ref=out_s.at[side, slot],
            dst_ref=in_s.at[side, lists - 1 - slot],
            send_sem=s_send.at[side, slot],
            recv_sem=s_recv.at[side, lists - 1 - slot],
            device_id=flux_peer(side, slot),
            device_id_type=MESH,
        )

    def sum_wait(side, slot):
        return pltpu.make_async_remote_copy(
            src_ref=out_s.at[side, lists - 1 - slot],
            dst_ref=in_s.at[side, slot],
            send_sem=s_send.at[side, lists - 1 - slot],
            recv_sem=s_recv.at[side, slot],
            device_id=flux_peer(side, slot),
            device_id_type=MESH,
        )

    def weight_copy(slot):
        return pltpu.make_async_remote_copy(
            src_ref=out_t.at[slot],
            dst_ref=in_t.at[lists - 1 - slot],
            send_sem=t_send.at[slot],
            recv_sem=t_recv.at[lists - 1 - slot],
            device_id={"cells": part + offsets[slot]},
            device_id_type=MESH,
        )

    def weight_wait(slot):
        return pltpu.make_async_remote_copy(
            src_ref=out_t.at[lists - 1 - slot],
            dst_ref=in_t.at[slot],
            send_sem=t_send.at[lists - 1 - slot],
            recv_sem=t_recv.at[slot],
            device_id={"cells": part + offsets[slot]},
            device_id_type=MESH,
        )

    def pair_copy(member):
        return pltpu.make_async_remote_copy(
            src_ref=pair.at[:, half_of(member)],
            dst_ref=pair.at[:, half_of(member)],
            send_sem=pair_send.at[0],
            recv_sem=pair_recv.at[0],
            device_id={"modes": partner},
            device_id_type=MESH,
        )

    def weight_copy(slot):
        return pltpu.make_async_remote_copy(
            src_ref=out_t.at[slot],
            dst_ref=in_t.at[lists - 1 - slot],
            send_sem=t_send.at[slot],
            recv_sem=t_recv.at[lists - 1 - slot],
            device_id={"cells": part + offsets[slot]},
            device_id_type=MESH,
        )

    def weight_wait(slot):
        return pltpu.make_async_remote_copy(
            src_ref=out_t.at[lists - 1 - slot],
            dst_ref=in_t.at[slot],
            send_sem=t_send.at[lists - 1 - slot],
            recv_sem=t_recv.at[slot],
            device_id={"cells": part + offsets[slot]},
            device_id_type=MESH,
        )

    loads = []
    for index, (source, target) in enumerate(
        [(faces_in, faces), (trans_in, trans), (sends_in, sends)]
        + [
            (pressure.at[:, chunk * BLOCK:(chunk + 1) * BLOCK], fields.at[0, chunk, mine])
            for chunk in range(chunks)
        ]
        + [(coupling_in, pair.at[:, half_of(group)]), (coupling_in, coupling), (storage_in, storage)]
    ):
        loads.append(pltpu.make_async_copy(source, target, load.at[index]))
    for copy in loads:
        copy.start()
    in_w[...] = jnp.zeros_like(in_w)
    in_s[...] = jnp.zeros_like(in_s)
    in_t[...] = jnp.zeros_like(in_t)
    barrier = pltpu.get_barrier_semaphore()
    for peer in (partner, far):
        pl.semaphore_signal(barrier, inc=1, device_id={"modes": peer}, device_id_type=MESH)
    peers = 2
    for slot in range(lists):
        peers = peers + 3 * present(slot).astype(jnp.int32)

        @pl.when(present(slot))
        def _():
            pl.semaphore_signal(
                barrier, inc=1, device_id={"cells": part + offsets[slot]}, device_id_type=MESH
            )
            for peer in (partner, far):
                pl.semaphore_signal(
                    barrier, inc=1, device_id={"cells": part + offsets[slot], "modes": peer}, device_id_type=MESH
                )
    def build_sends(base):
        for slot in range(lists):
            hot = onehot(BLOCK, base, sends[0, slot:slot + 1])
            wide[base:base + BLOCK, slot * width:(slot + 1) * width] = jnp.where(hot, one, zero)

    half = 2 * rows
    near_half = pl.ds(pl.multiple_of(lax.div(group, 2) * half, half), half)
    far_half = pl.ds(pl.multiple_of((1 - lax.div(group, 2)) * half, half), half)

    def build_faces(index, carry):
        at = pl.ds(pl.multiple_of(index * TILE, TILE), TILE)
        to = pl.ds(pl.multiple_of(ghosts + index * TILE, TILE), TILE)
        for chunk in range(chunks):
            base = chunk * BLOCK
            plus = onehot(BLOCK, base, faces[0:1, at])
            minus = onehot(BLOCK, base, faces[1:2, at])
            signs = jnp.where(plus, one, jnp.where(minus, -one, zero))
            wide[base:base + BLOCK, to] = signs
            tall[at, base:base + BLOCK] = signs.T
            part_sum = jnp.dot(fields[0, chunk, near_half], signs, preferred_element_type=jnp.float32)
            total = part_sum if chunk == 0 else total + part_sum
        diff[near_half, at] = total.astype(jnp.bfloat16)
        return carry

    def build_ghost(index, carry):
        at = pl.ds(pl.multiple_of(index * TILE, TILE), TILE)
        other = faces[1:2, at]
        for base in range(0, ghosts, BLOCK):
            hot = onehot(BLOCK, cells + base, other)
            ghost_hot[base:base + BLOCK, at] = jnp.where(hot, one, zero)
        return carry

    def find_slots():
        t = trans[...]
        t_high = t.astype(jnp.bfloat16)
        t_low = (t - t_high.astype(jnp.float32)).astype(jnp.bfloat16)
        picked_rows[...] = jnp.zeros_like(picked_rows)
        picked_rows[0:terms] = t_high
        picked_rows[16:16 + terms] = t_low
        owner_next = faces[0:1] + 1
        picked_rows[32:33] = (owner_next // 32).astype(jnp.float32).astype(jnp.bfloat16)
        picked_rows[33:34] = (owner_next % 32).astype(jnp.float32).astype(jnp.bfloat16)
        lax.fori_loop(0, face_count // TILE, build_ghost, 0)

    def weigh_slots():
        found = lax.dot_general(
            picked_rows[...], ghost_hot[...], (((1,), (1,)), ((), ())), preferred_element_type=jnp.float32
        )
        slot_weights[...] = found[0:16] + found[16:32]
        slot_owner[0:1] = (found[32:33] * 32.0 + found[33:34] - 1.0).astype(jnp.int32)
        for slot in range(lists):
            out_t[slot] = slot_weights[:, slot * width:(slot + 1) * width]

    def build_owners():
        for base in range(0, cells, BLOCK):
            hot = onehot(BLOCK, base, slot_owner[0:1])
            tall[face_count:, base:base + BLOCK] = jnp.where(hot, -one, zero).T

    def differ(app, chunk, members):
        rows_of = slice(chunk * BLOCK, (chunk + 1) * BLOCK)
        field = fields[app, chunk, members]
        for start in range(0, face_count, WIDE):
            at = slice(start, start + WIDE)
            total = jnp.dot(
                field, wide[rows_of, ghosts + start:ghosts + start + WIDE], preferred_element_type=jnp.float32
            )
            if chunk > 0:
                total += sums[:, at]
            if chunk < chunks - 1:
                sums[:, at] = total
            else:
                diff[members, at] = total.astype(jnp.bfloat16)

    def pick(app, members):
        total = jnp.dot(fields[app, 0, members], wide[0:BLOCK, 0:ghosts], preferred_element_type=jnp.float32)
        for chunk in range(1, chunks):
            total += jnp.dot(
                fields[app, chunk, members], wide[chunk * BLOCK:(chunk + 1) * BLOCK, 0:ghosts],
                preferred_element_type=jnp.float32,
            )
        return total.astype(jnp.bfloat16)

    def send_ghosts():
        total = pick(0, mine)
        for slot in range(lists):
            out_w[slot] = total[:, slot * width:(slot + 1) * width]

            @pl.when(present(slot))
            def _():
                for side in range(2):
                    ghost_copy(side, slot).start()

    def send_sums():
        ghost = pick(1, near_half)
        for slot in range(lists):
            @pl.when(present(slot))
            def _():
                weight_wait(slot).wait_recv()
        weights = jnp.concatenate([in_t[slot] for slot in range(lists)], axis=1)
        for side, member in ((1, far), (0, group)):
            sent = mix(turned[:, band(member)].reshape(terms * rows, half), ghost, weights)
            for slot in range(lists):
                out_s[side, slot] = sent[:, slot * width:(slot + 1) * width].astype(jnp.bfloat16)

                @pl.when(present(slot))
                def _():
                    sum_copy(side, slot).start()

    def mix_ghosts():
        for slot in range(lists):
            @pl.when(present(slot))
            def _():
                for side in range(2):
                    ghost_wait(side, slot).wait_recv()
        ghost = jnp.concatenate([in_w[slot] for slot in range(lists)], axis=1)
        for member in (far, group):
            sent = mix(turned[:, band(member)].reshape(terms * rows, half), ghost, slot_weights[...])
            if member is far:
                out_f[...] = sent.astype(jnp.bfloat16)
                flux_copy().start()
            else:
                fluxes[0:rows] = sent.astype(jnp.bfloat16)

    def pass_on(app, chunk):
        far_copy(app, chunk, far).wait_recv()
        pass_copy(app, chunk).start()

    def mix(stacked, column, weights):
        mixed = jnp.dot(stacked, column, preferred_element_type=jnp.float32)
        total = mixed[0:rows] * weights[0:1]
        for term in range(1, terms):
            total += mixed[term * rows:(term + 1) * rows] * weights[term:term + 1]
        return total

    for copy in loads[:3]:
        copy.wait()
    find_slots()
    for copy in loads[3:]:
        copy.wait()
    pl.semaphore_wait(barrier, peers)
    for chunk in range(chunks):
        far_copy(0, chunk).start()
        near_copy(0, chunk).start()
    pair_copy(group).start()
    for chunk in range(chunks):
        build_sends(chunk * BLOCK)
    send_ghosts()
    weigh_slots()
    for slot in range(lists):
        @pl.when(present(slot))
        def _():
            weight_copy(slot).start()
    for chunk in range(chunks):
        near_copy(0, chunk, partner).wait_recv()
    lax.fori_loop(0, face_count // TILE, build_faces, 0, unroll=True)
    pair_copy(partner).wait_recv()
    for term in range(terms):
        turned[term] = pair[term].T
    for app, target in enumerate((first, second)):
        if app == 1:
            for chunk in range(chunks):
                near_copy(app, chunk, partner).wait_recv()
            send_sums()
        for chunk in range(chunks):
            pass_on(app, chunk)
            if app == 1:
                differ(app, chunk, near_half)
        if app == 0:
            mix_ghosts()
            build_owners()
        for chunk in range(chunks):
            pass_copy(app, chunk, far_partner).wait_recv()
            differ(app, chunk, far_half)

        stacked = coupling[...].reshape(terms * rows, groups * rows)
        for start in range(0, face_count, TILE):
            at = slice(start, start + TILE)
            total = mix(stacked, diff[:, at], trans[:, at])
            high = total.astype(jnp.bfloat16)
            flux[0:rows, at] = high
            flux[rows:2 * rows, at] = (total - high.astype(jnp.float32)).astype(jnp.bfloat16)

        def inner(chunk):
            span = slice(chunk * BLOCK, (chunk + 2) * BLOCK)
            spread = jnp.dot(flux[...], tall[0:face_count, span], preferred_element_type=jnp.float32)
            own = jnp.concatenate([fields[app, chunk, mine], fields[app, chunk + 1, mine]], axis=1)
            image = storage[:, span] * own.astype(jnp.float32)
            totals[:, span] = image + spread[0:rows] + spread[rows:2 * rows]

        def finish(chunk):
            span = slice(chunk * BLOCK, (chunk + 1) * BLOCK)
            spread = jnp.dot(arrived, tall[face_count:, span], preferred_element_type=jnp.float32)
            image = (totals[:, span] + (spread[0:rows] + spread[rows:half])).astype(jnp.bfloat16)
            target[:, span] = image
            if app == 0:
                fields[1, chunk, mine, :] = image
                far_copy(1, chunk).start()
                near_copy(1, chunk).start()

        inner(0)
        if app == 0:
            flux_copy().wait_recv()
            arrived = fluxes[...]
        else:
            for slot in range(lists):
                @pl.when(present(slot))
                def _():
                    for side in range(2):
                        sum_wait(side, slot).wait_recv()
            arrived = jnp.concatenate(
                [jnp.concatenate([in_s[side, slot] for slot in range(lists)], axis=1) for side in range(2)], axis=0
            )
        for chunk in range(chunks):
            if chunk > 0 and chunk % 2 == 0:
                inner(chunk)
            finish(chunk)

    for app in range(2):
        for chunk in range(chunks):
            far_copy(app, chunk).wait_send()
            near_copy(app, chunk).wait_send()
            pass_copy(app, chunk).wait_send()
    flux_copy().wait_send()
    for slot in range(lists):
        @pl.when(present(slot))
        def _():
            weight_copy(slot).wait_send()
            for side in range(2):
                ghost_copy(side, slot).wait_send()
                sum_copy(side, slot).wait_send()
    pair_copy(group).wait_send()


def write_out(first_in, second_in, first, second, done):
    copies = [
        pltpu.make_async_copy(source, target, done.at[index])
        for index, (source, target) in enumerate(((first_in, first), (second_in, second)))
    ]
    for copy in copies:
        copy.start()
    for copy in copies:
        copy.wait()


def local(parts, groups, pressure, storage, coupling, trans, face_cells, send_list):
    assert groups == 4
    rows, cells = pressure.shape
    face_count = face_cells.shape[1]
    lists, width = send_list.shape[1:]
    ghosts = lists * width
    chunks = cells // BLOCK
    bf16 = jnp.bfloat16
    vmem = pl.BlockSpec(memory_space=pltpu.VMEM)
    image = jax.ShapeDtypeStruct((rows, cells), bf16)
    images = pl.pallas_call(
        functools.partial(kernel, parts, groups),
        out_shape=(pltpu.VMEM((rows, cells), bf16), pltpu.VMEM((rows, cells), bf16)),
        in_specs=[pl.BlockSpec(memory_space=pltpu.HBM)] * 6,
        out_specs=(vmem, vmem),
        scratch_shapes=[
            pltpu.VMEM((1, cells), jnp.float32),
            pltpu.VMEM(coupling.shape, bf16),
            pltpu.VMEM(trans.shape, jnp.float32),
            pltpu.VMEM(face_cells.shape, jnp.int32),
            pltpu.VMEM(send_list.shape, jnp.int32),
            pltpu.VMEM((coupling.shape[0], 2 * rows, groups * rows), bf16),
            pltpu.VMEM((coupling.shape[0], groups * rows, 2 * rows), bf16),
            pltpu.VMEM((cells, ghosts + face_count), bf16),
            pltpu.VMEM((face_count + ghosts, cells), bf16),
            pltpu.VMEM((ghosts, face_count), bf16),
            pltpu.VMEM((48, face_count), bf16),
            pltpu.VMEM((2, chunks, groups * rows, BLOCK), bf16),
            pltpu.VMEM((2 * rows, face_count), jnp.float32),
            pltpu.VMEM((groups * rows, face_count), bf16),
            pltpu.VMEM((rows, cells), jnp.float32),
            pltpu.VMEM((2 * rows, face_count), bf16),
            pltpu.VMEM((lists, rows, width), bf16),
            pltpu.VMEM((lists, 2 * rows, width), bf16),
            pltpu.VMEM((16, ghosts), jnp.float32),
            pltpu.VMEM((8, ghosts), jnp.int32),
            pltpu.VMEM((2 * rows, ghosts), bf16),
            pltpu.VMEM((rows, ghosts), bf16),
            pltpu.VMEM((2, lists, rows, width), bf16),
            pltpu.VMEM((2, lists, rows, width), bf16),
            pltpu.VMEM((lists, 16, width), jnp.float32),
            pltpu.VMEM((lists, 16, width), jnp.float32),
            pltpu.SemaphoreType.DMA((chunks + 6,)),
        ]
        + [pltpu.SemaphoreType.DMA((2, chunks))] * 6
        + [pltpu.SemaphoreType.DMA((2, lists))] * 2
        + [pltpu.SemaphoreType.DMA((1,))] * 4
        + [pltpu.SemaphoreType.DMA((2, lists))] * 2
        + [pltpu.SemaphoreType.DMA((lists,))] * 2,
        compiler_params=pltpu.CompilerParams(
            collective_id=0, has_side_effects=True, vmem_limit_bytes=61 * 1024 * 1024
        ),
    )(pressure, storage.reshape(1, cells), coupling, trans, face_cells, send_list)
    hbm = pl.BlockSpec(memory_space=pltpu.HBM)
    return pl.pallas_call(
        write_out,
        out_shape=(image, image),
        in_specs=[vmem] * 2,
        out_specs=(hbm, hbm),
        scratch_shapes=[pltpu.SemaphoreType.DMA((2,))],
        compiler_params=pltpu.CompilerParams(vmem_limit_bytes=1024 * 1024),
    )(*images)


def solution(mesh):
    placed = (
        P("modes", "cells"),
        P("cells"),
        P(None, "modes", None),
        P(None, "cells"),
        P(None, "cells"),
        P("cells", None, None),
    )
    return jax.shard_map(
        functools.partial(local, mesh.shape["cells"], mesh.shape["modes"]),
        mesh=mesh,
        in_specs=placed,
        out_specs=(P("modes", "cells"), P("modes", "cells")),
        check_vma=False,
    )
```

```python
import functools

import jax
import jax.numpy as jnp
from jax import lax
from jax.experimental import pallas as pl
from jax.experimental.pallas import tpu as pltpu
from jax.sharding import PartitionSpec as P

MESH = pl.DeviceIdType.MESH
BLOCK = 256
TILE = 512
WIDE = 1536


def onehot(rows, base, index_row, dtype=jnp.bfloat16):
    near = jnp.clip(index_row - base, -1, rows).astype(jnp.float32).astype(jnp.bfloat16)
    iota = lax.broadcasted_iota(jnp.int32, (rows, index_row.shape[1]), 0)
    return iota.astype(jnp.float32).astype(jnp.bfloat16) == near


def kernel(
    parts, groups, pressure, storage_in, coupling_in, trans_in, faces_in, sends_in, first, second,
    storage, coupling, trans, faces, sends, pair, turned,
    wide, tall, ghost_hot, picked_rows, fields, sums, diff, totals, flux, out_w, in_w, slot_weights, slot_owner, fluxes, out_f,
    out_s, in_s, out_t, in_t,
    load, near_send, near_recv, far_send, far_recv, pass_send, pass_recv,
    w_send, w_recv, f_send, f_recv, pair_send, pair_recv, s_send, s_recv,
    t_send, t_recv,
):
    rows, cells = pressure.shape
    terms = coupling.shape[0]
    face_count = faces.shape[1]
    lists, width = sends.shape[1:]
    ghosts = lists * width
    reach = lists // 2
    offsets = list(range(-reach, 0)) + list(range(1, reach + 1))
    chunks = cells // BLOCK
    part = lax.axis_index("cells")
    group = lax.axis_index("modes")
    partner = group + 1 - 2 * lax.rem(group, 2)
    far = lax.rem(group + 2, 4)
    far_partner = lax.rem(partner + 2, 4)

    def band(member):
        return pl.ds(pl.multiple_of(member * rows, rows), rows)

    mine = band(group)
    one = jnp.ones((), jnp.bfloat16)
    zero = jnp.zeros((), jnp.bfloat16)

    def present(slot):
        return jnp.logical_and(part + offsets[slot] >= 0, part + offsets[slot] < parts)

    def band_copy(app, chunk, member, send_sem, recv_sem, target):
        return pltpu.make_async_remote_copy(
            src_ref=fields.at[app, chunk, band(member)],
            dst_ref=fields.at[app, chunk, band(member)],
            send_sem=send_sem.at[app, chunk],
            recv_sem=recv_sem.at[app, chunk],
            device_id={"modes": target},
            device_id_type=MESH,
        )

    def near_copy(app, chunk, member=group):
        return band_copy(app, chunk, member, near_send, near_recv, partner)

    def far_copy(app, chunk, member=group):
        return band_copy(app, chunk, member, far_send, far_recv, far)

    def pass_copy(app, chunk, member=far):
        return band_copy(app, chunk, member, pass_send, pass_recv, partner)

    def ghost_peer(side, slot):
        peer = part + offsets[slot]
        return {"cells": peer} if side == 0 else {"cells": peer, "modes": partner}

    def half_of(member):
        return pl.ds(pl.multiple_of(lax.rem(member, 2) * rows, rows), rows)

    def ghost_copy(side, slot):
        return pltpu.make_async_remote_copy(
            src_ref=out_w.at[slot],
            dst_ref=in_w.at[lists - 1 - slot, half_of(group)],
            send_sem=w_send.at[side, slot],
            recv_sem=w_recv.at[side, lists - 1 - slot],
            device_id=ghost_peer(side, slot),
            device_id_type=MESH,
        )

    def ghost_wait(side, slot):
        return pltpu.make_async_remote_copy(
            src_ref=out_w.at[lists - 1 - slot],
            dst_ref=in_w.at[slot, half_of(group if side == 0 else partner)],
            send_sem=w_send.at[side, lists - 1 - slot],
            recv_sem=w_recv.at[side, slot],
            device_id=ghost_peer(side, slot),
            device_id_type=MESH,
        )

    def flux_copy():
        return pltpu.make_async_remote_copy(
            src_ref=out_f,
            dst_ref=fluxes.at[rows:2 * rows],
            send_sem=f_send.at[0],
            recv_sem=f_recv.at[0],
            device_id={"modes": far},
            device_id_type=MESH,
        )

    def flux_peer(side, slot):
        peer = part + offsets[slot]
        return {"cells": peer} if side == 0 else {"cells": peer, "modes": far}

    def sum_copy(side, slot):
        return pltpu.make_async_remote_copy(
            src_ref=out_s.at[side, slot],
            dst_ref=in_s.at[side, lists - 1 - slot],
            send_sem=s_send.at[side, slot],
            recv_sem=s_recv.at[side, lists - 1 - slot],
            device_id=flux_peer(side, slot),
            device_id_type=MESH,
        )

    def sum_wait(side, slot):
        return pltpu.make_async_remote_copy(
            src_ref=out_s.at[side, lists - 1 - slot],
            dst_ref=in_s.at[side, slot],
            send_sem=s_send.at[side, lists - 1 - slot],
            recv_sem=s_recv.at[side, slot],
            device_id=flux_peer(side, slot),
            device_id_type=MESH,
        )

    def weight_copy(slot):
        return pltpu.make_async_remote_copy(
            src_ref=out_t.at[slot],
            dst_ref=in_t.at[lists - 1 - slot],
            send_sem=t_send.at[slot],
            recv_sem=t_recv.at[lists - 1 - slot],
            device_id={"cells": part + offsets[slot]},
            device_id_type=MESH,
        )

    def weight_wait(slot):
        return pltpu.make_async_remote_copy(
            src_ref=out_t.at[lists - 1 - slot],
            dst_ref=in_t.at[slot],
            send_sem=t_send.at[lists - 1 - slot],
            recv_sem=t_recv.at[slot],
            device_id={"cells": part + offsets[slot]},
            device_id_type=MESH,
        )

    def pair_copy(member):
        return pltpu.make_async_remote_copy(
            src_ref=pair.at[:, half_of(member)],
            dst_ref=pair.at[:, half_of(member)],
            send_sem=pair_send.at[0],
            recv_sem=pair_recv.at[0],
            device_id={"modes": partner},
            device_id_type=MESH,
        )

    def weight_copy(slot):
        return pltpu.make_async_remote_copy(
            src_ref=out_t.at[slot],
            dst_ref=in_t.at[lists - 1 - slot],
            send_sem=t_send.at[slot],
            recv_sem=t_recv.at[lists - 1 - slot],
            device_id={"cells": part + offsets[slot]},
            device_id_type=MESH,
        )

    def weight_wait(slot):
        return pltpu.make_async_remote_copy(
            src_ref=out_t.at[lists - 1 - slot],
            dst_ref=in_t.at[slot],
            send_sem=t_send.at[lists - 1 - slot],
            recv_sem=t_recv.at[slot],
            device_id={"cells": part + offsets[slot]},
            device_id_type=MESH,
        )

    loads = []
    for index, (source, target) in enumerate(
        [(faces_in, faces), (trans_in, trans), (sends_in, sends)]
        + [
            (pressure.at[:, chunk * BLOCK:(chunk + 1) * BLOCK], fields.at[0, chunk, mine])
            for chunk in range(chunks)
        ]
        + [(coupling_in, pair.at[:, half_of(group)]), (coupling_in, coupling), (storage_in, storage)]
    ):
        loads.append(pltpu.make_async_copy(source, target, load.at[index]))
    for copy in loads:
        copy.start()
    in_w[...] = jnp.zeros_like(in_w)
    in_s[...] = jnp.zeros_like(in_s)
    in_t[...] = jnp.zeros_like(in_t)
    barrier = pltpu.get_barrier_semaphore()
    for peer in (partner, far):
        pl.semaphore_signal(barrier, inc=1, device_id={"modes": peer}, device_id_type=MESH)
    peers = 2
    for slot in range(lists):
        peers = peers + 3 * present(slot).astype(jnp.int32)

        @pl.when(present(slot))
        def _():
            pl.semaphore_signal(
                barrier, inc=1, device_id={"cells": part + offsets[slot]}, device_id_type=MESH
            )
            for peer in (partner, far):
                pl.semaphore_signal(
                    barrier, inc=1, device_id={"cells": part + offsets[slot], "modes": peer}, device_id_type=MESH
                )
    def build_sends(base):
        for slot in range(lists):
            hot = onehot(BLOCK, base, sends[0, slot:slot + 1])
            wide[base:base + BLOCK, slot * width:(slot + 1) * width] = jnp.where(hot, one, zero)

    half = 2 * rows
    near_half = pl.ds(pl.multiple_of(lax.div(group, 2) * half, half), half)
    far_half = pl.ds(pl.multiple_of((1 - lax.div(group, 2)) * half, half), half)

    def build_faces(index, carry):
        at = pl.ds(pl.multiple_of(index * TILE, TILE), TILE)
        to = pl.ds(pl.multiple_of(ghosts + index * TILE, TILE), TILE)
        for chunk in range(chunks):
            base = chunk * BLOCK
            plus = onehot(BLOCK, base, faces[0:1, at])
            minus = onehot(BLOCK, base, faces[1:2, at])
            signs = jnp.where(plus, one, jnp.where(minus, -one, zero))
            wide[base:base + BLOCK, to] = signs
            tall[at, base:base + BLOCK] = signs.T
            part_sum = jnp.dot(fields[0, chunk, near_half], signs, preferred_element_type=jnp.float32)
            total = part_sum if chunk == 0 else total + part_sum
        diff[near_half, at] = total.astype(jnp.bfloat16)
        return carry

    def build_ghost(index, carry):
        at = pl.ds(pl.multiple_of(index * TILE, TILE), TILE)
        other = faces[1:2, at]
        for base in range(0, ghosts, BLOCK):
            hot = onehot(BLOCK, cells + base, other)
            ghost_hot[base:base + BLOCK, at] = jnp.where(hot, one, zero)
        return carry

    def find_slots():
        t = trans[...]
        t_high = t.astype(jnp.bfloat16)
        t_low = (t - t_high.astype(jnp.float32)).astype(jnp.bfloat16)
        picked_rows[...] = jnp.zeros_like(picked_rows)
        picked_rows[0:terms] = t_high
        picked_rows[16:16 + terms] = t_low
        owner_next = faces[0:1] + 1
        picked_rows[32:33] = (owner_next // 32).astype(jnp.float32).astype(jnp.bfloat16)
        picked_rows[33:34] = (owner_next % 32).astype(jnp.float32).astype(jnp.bfloat16)
        lax.fori_loop(0, face_count // TILE, build_ghost, 0)

    def weigh_slots():
        found = lax.dot_general(
            picked_rows[...], ghost_hot[...], (((1,), (1,)), ((), ())), preferred_element_type=jnp.float32
        )
        slot_weights[...] = found[0:16] + found[16:32]
        slot_owner[0:1] = (found[32:33] * 32.0 + found[33:34] - 1.0).astype(jnp.int32)
        for slot in range(lists):
            out_t[slot] = slot_weights[:, slot * width:(slot + 1) * width]

    def build_owners():
        for base in range(0, cells, BLOCK):
            hot = onehot(BLOCK, base, slot_owner[0:1])
            tall[face_count:, base:base + BLOCK] = jnp.where(hot, -one, zero).T

    def differ(app, chunk, members):
        rows_of = slice(chunk * BLOCK, (chunk + 1) * BLOCK)
        field = fields[app, chunk, members]
        for start in range(0, face_count, WIDE):
            at = slice(start, start + WIDE)
            total = jnp.dot(
                field, wide[rows_of, ghosts + start:ghosts + start + WIDE], preferred_element_type=jnp.float32
            )
            if chunk > 0:
                total += sums[:, at]
            if chunk < chunks - 1:
                sums[:, at] = total
            else:
                diff[members, at] = total.astype(jnp.bfloat16)

    def pick(app, members):
        total = jnp.dot(fields[app, 0, members], wide[0:BLOCK, 0:ghosts], preferred_element_type=jnp.float32)
        for chunk in range(1, chunks):
            total += jnp.dot(
                fields[app, chunk, members], wide[chunk * BLOCK:(chunk + 1) * BLOCK, 0:ghosts],
                preferred_element_type=jnp.float32,
            )
        return total.astype(jnp.bfloat16)

    def send_ghosts():
        total = pick(0, mine)
        for slot in range(lists):
            out_w[slot] = total[:, slot * width:(slot + 1) * width]

            @pl.when(present(slot))
            def _():
                for side in range(2):
                    ghost_copy(side, slot).start()

    def send_sums():
        ghost = pick(1, near_half)
        for slot in range(lists):
            @pl.when(present(slot))
            def _():
                weight_wait(slot).wait_recv()
        weights = jnp.concatenate([in_t[slot] for slot in range(lists)], axis=1)
        for side, member in ((1, far), (0, group)):
            sent = mix(turned[:, band(member)].reshape(terms * rows, half), ghost, weights)
            for slot in range(lists):
                out_s[side, slot] = sent[:, slot * width:(slot + 1) * width].astype(jnp.bfloat16)

                @pl.when(present(slot))
                def _():
                    sum_copy(side, slot).start()

    def mix_ghosts():
        for slot in range(lists):
            @pl.when(present(slot))
            def _():
                for side in range(2):
                    ghost_wait(side, slot).wait_recv()
        ghost = jnp.concatenate([in_w[slot] for slot in range(lists)], axis=1)
        for member in (far, group):
            sent = mix(turned[:, band(member)].reshape(terms * rows, half), ghost, slot_weights[...])
            if member is far:
                out_f[...] = sent.astype(jnp.bfloat16)
                flux_copy().start()
            else:
                fluxes[0:rows] = sent.astype(jnp.bfloat16)

    def pass_on(app, chunk):
        far_copy(app, chunk, far).wait_recv()
        pass_copy(app, chunk).start()

    def mix(stacked, column, weights):
        mixed = jnp.dot(stacked, column, preferred_element_type=jnp.float32)
        total = mixed[0:rows] * weights[0:1]
        for term in range(1, terms):
            total += mixed[term * rows:(term + 1) * rows] * weights[term:term + 1]
        return total

    for copy in loads[:3]:
        copy.wait()
    find_slots()
    for copy in loads[3:]:
        copy.wait()
    pl.semaphore_wait(barrier, peers)
    for chunk in range(chunks):
        far_copy(0, chunk).start()
        near_copy(0, chunk).start()
    pair_copy(group).start()
    for chunk in range(chunks):
        build_sends(chunk * BLOCK)
    send_ghosts()
    weigh_slots()
    for slot in range(lists):
        @pl.when(present(slot))
        def _():
            weight_copy(slot).start()
    for chunk in range(chunks):
        near_copy(0, chunk, partner).wait_recv()
    lax.fori_loop(0, face_count // TILE, build_faces, 0, unroll=True)
    pair_copy(partner).wait_recv()
    for term in range(terms):
        turned[term] = pair[term].T
    for app, target in enumerate((first, second)):
        if app == 1:
            for chunk in range(chunks):
                near_copy(app, chunk, partner).wait_recv()
            send_sums()
        for chunk in range(chunks):
            pass_on(app, chunk)
            if app == 1:
                differ(app, chunk, near_half)
        if app == 0:
            mix_ghosts()
            build_owners()
        for chunk in range(chunks):
            pass_copy(app, chunk, far_partner).wait_recv()
            differ(app, chunk, far_half)

        stacked = coupling[...].reshape(terms * rows, groups * rows)
        for start in range(0, face_count, WIDE):
            at = slice(start, start + WIDE)
            total = mix(stacked, diff[:, at], trans[:, at])
            high = total.astype(jnp.bfloat16)
            flux[0:rows, at] = high
            flux[rows:2 * rows, at] = (total - high.astype(jnp.float32)).astype(jnp.bfloat16)

        def inner(chunk):
            span = slice(chunk * BLOCK, (chunk + 2) * BLOCK)
            spread = jnp.dot(flux[...], tall[0:face_count, span], preferred_element_type=jnp.float32)
            own = jnp.concatenate([fields[app, chunk, mine], fields[app, chunk + 1, mine]], axis=1)
            image = storage[:, span] * own.astype(jnp.float32)
            totals[:, span] = image + spread[0:rows] + spread[rows:2 * rows]

        def finish(chunk):
            span = slice(chunk * BLOCK, (chunk + 1) * BLOCK)
            spread = jnp.dot(arrived, tall[face_count:, span], preferred_element_type=jnp.float32)
            image = (totals[:, span] + (spread[0:rows] + spread[rows:half])).astype(jnp.bfloat16)
            target[:, span] = image
            if app == 0:
                fields[1, chunk, mine, :] = image
                far_copy(1, chunk).start()
                near_copy(1, chunk).start()

        inner(0)
        if app == 0:
            flux_copy().wait_recv()
            arrived = fluxes[...]
        else:
            for slot in range(lists):
                @pl.when(present(slot))
                def _():
                    for side in range(2):
                        sum_wait(side, slot).wait_recv()
            arrived = jnp.concatenate(
                [jnp.concatenate([in_s[side, slot] for slot in range(lists)], axis=1) for side in range(2)], axis=0
            )
        for chunk in range(chunks):
            if chunk > 0 and chunk % 2 == 0:
                inner(chunk)
            finish(chunk)

    for app in range(2):
        for chunk in range(chunks):
            far_copy(app, chunk).wait_send()
            near_copy(app, chunk).wait_send()
            pass_copy(app, chunk).wait_send()
    flux_copy().wait_send()
    for slot in range(lists):
        @pl.when(present(slot))
        def _():
            weight_copy(slot).wait_send()
            for side in range(2):
                ghost_copy(side, slot).wait_send()
                sum_copy(side, slot).wait_send()
    pair_copy(group).wait_send()


def write_out(first_in, second_in, first, second, done):
    copies = [
        pltpu.make_async_copy(source, target, done.at[index])
        for index, (source, target) in enumerate(((first_in, first), (second_in, second)))
    ]
    for copy in copies:
        copy.start()
    for copy in copies:
        copy.wait()


def local(parts, groups, pressure, storage, coupling, trans, face_cells, send_list):
    assert groups == 4
    rows, cells = pressure.shape
    face_count = face_cells.shape[1]
    lists, width = send_list.shape[1:]
    ghosts = lists * width
    chunks = cells // BLOCK
    bf16 = jnp.bfloat16
    vmem = pl.BlockSpec(memory_space=pltpu.VMEM)
    image = jax.ShapeDtypeStruct((rows, cells), bf16)
    images = pl.pallas_call(
        functools.partial(kernel, parts, groups),
        out_shape=(pltpu.VMEM((rows, cells), bf16), pltpu.VMEM((rows, cells), bf16)),
        in_specs=[pl.BlockSpec(memory_space=pltpu.HBM)] * 6,
        out_specs=(vmem, vmem),
        scratch_shapes=[
            pltpu.VMEM((1, cells), jnp.float32),
            pltpu.VMEM(coupling.shape, bf16),
            pltpu.VMEM(trans.shape, jnp.float32),
            pltpu.VMEM(face_cells.shape, jnp.int32),
            pltpu.VMEM(send_list.shape, jnp.int32),
            pltpu.VMEM((coupling.shape[0], 2 * rows, groups * rows), bf16),
            pltpu.VMEM((coupling.shape[0], groups * rows, 2 * rows), bf16),
            pltpu.VMEM((cells, ghosts + face_count), bf16),
            pltpu.VMEM((face_count + ghosts, cells), bf16),
            pltpu.VMEM((ghosts, face_count), bf16),
            pltpu.VMEM((48, face_count), bf16),
            pltpu.VMEM((2, chunks, groups * rows, BLOCK), bf16),
            pltpu.VMEM((2 * rows, face_count), jnp.float32),
            pltpu.VMEM((groups * rows, face_count), bf16),
            pltpu.VMEM((rows, cells), jnp.float32),
            pltpu.VMEM((2 * rows, face_count), bf16),
            pltpu.VMEM((lists, rows, width), bf16),
            pltpu.VMEM((lists, 2 * rows, width), bf16),
            pltpu.VMEM((16, ghosts), jnp.float32),
            pltpu.VMEM((8, ghosts), jnp.int32),
            pltpu.VMEM((2 * rows, ghosts), bf16),
            pltpu.VMEM((rows, ghosts), bf16),
            pltpu.VMEM((2, lists, rows, width), bf16),
            pltpu.VMEM((2, lists, rows, width), bf16),
            pltpu.VMEM((lists, 16, width), jnp.float32),
            pltpu.VMEM((lists, 16, width), jnp.float32),
            pltpu.SemaphoreType.DMA((chunks + 6,)),
        ]
        + [pltpu.SemaphoreType.DMA((2, chunks))] * 6
        + [pltpu.SemaphoreType.DMA((2, lists))] * 2
        + [pltpu.SemaphoreType.DMA((1,))] * 4
        + [pltpu.SemaphoreType.DMA((2, lists))] * 2
        + [pltpu.SemaphoreType.DMA((lists,))] * 2,
        compiler_params=pltpu.CompilerParams(
            collective_id=0, has_side_effects=True, vmem_limit_bytes=61 * 1024 * 1024
        ),
    )(pressure, storage.reshape(1, cells), coupling, trans, face_cells, send_list)
    hbm = pl.BlockSpec(memory_space=pltpu.HBM)
    return pl.pallas_call(
        write_out,
        out_shape=(image, image),
        in_specs=[vmem] * 2,
        out_specs=(hbm, hbm),
        scratch_shapes=[pltpu.SemaphoreType.DMA((2,))],
        compiler_params=pltpu.CompilerParams(vmem_limit_bytes=1024 * 1024),
    )(*images)


def solution(mesh):
    placed = (
        P("modes", "cells"),
        P("cells"),
        P(None, "modes", None),
        P(None, "cells"),
        P(None, "cells"),
        P("cells", None, None),
    )
    return jax.shard_map(
        functools.partial(local, mesh.shape["cells"], mesh.shape["modes"]),
        mesh=mesh,
        in_specs=placed,
        out_specs=(P("modes", "cells"), P("modes", "cells")),
        check_vma=False,
    )
```
